32 devices in a mesh: text: 16 (over z, y, core), video: 2 (over x).
Axes of the slice: x: 2, y: 2, z: 4, core: 2. Of those that a mesh axis runs over, the one named last changes fastest.
Arguments:
- queries: bfloat16 [2048, 4096], P('text'), may hold values from -53 to 53
- video_keys: bfloat16 [512, 512], P('video'), may hold values from -6 to 6
- video_values: bfloat16 [512, 512], P('video'), may hold values from -6 to 6
- grad_out: bfloat16 [2048, 4096], P('text'), may hold values from -6 to 6
- positions: int32 [2048], P('text'), may hold values from 1 to 511, as said below
- span_bounds: int32 [16, 2], P('text'), may hold values from 0 to 512, as said below
Outputs:
- attended: bfloat16 [2048, 4096], P('text', 'video')
- grad_query: bfloat16 [2048, 4096], P('text', 'video')
- grad_key: bfloat16 [512, 512], P(('video', 'text'))
- grad_value: bfloat16 [512, 512], P(('video', 'text'))
The draws below stay inside these ranges and needn't reach their ends.
Inputs may be any that keep to these rules, and one draw needn't show every extreme that they name: `span_bounds`: column 0 is a multiple of 128 from 0 to 0; column 1 is a multiple of 128 from 512 to 512. `positions`: each position is at least its block's span start plus 1.
All inputs are finite; a program needn't handle non-finite values.
Results may differ from the reference program's by a relative error of at most 0.017.
Values sent between devices are 32-bit elements; how exact they have to be, the bound alone decides.
A program may use at most 128 MiB of HBM per device.

```python
import jax
import jax.numpy as jnp
from jax import lax

VID_DEV = 256
H = 32
G = 4
HD = 128
TBLK = 128
STEP = 128
TEXT = 2048
VTOK = 512
NBLK = 16
N_VIDEO = 2


def span_table(key):
    base_key = jax.random.fold_in(key, 101)
    key_lower, key_upper, key_reach = jax.random.split(base_key, 3)
    quarter = VTOK // (4 * STEP)
    lower = STEP * jax.random.randint(key_lower, (NBLK,), 0, quarter)
    upper = VTOK - STEP * jax.random.randint(key_upper, (NBLK,), 0, quarter)
    lower = lower.at[0].set(0).at[1].set(VTOK // 4 - STEP)
    upper = upper.at[0].set(VTOK).at[1].set(3 * VTOK // 4 + STEP)
    lower_rows = jnp.repeat(lower, TBLK)
    reach = jax.random.randint(key_reach, (TEXT,), 0, VTOK - lower_rows - 1)
    places = lower_rows + 1 + reach
    places = places.at[0].set(1).at[1].set(VTOK - 1)
    return (lower.astype(jnp.int32), upper.astype(jnp.int32), places.astype(jnp.int32))


def key_table(key):
    base_key = jax.random.fold_in(key, 202)
    table = jax.random.truncated_normal(base_key, -6.0, 6.0, (VTOK, G * HD), jnp.float32)
    return table


def draw_video_keys(key, part):
    return key_table(key).astype(jnp.bfloat16)


def draw_positions(key, part):
    lower, upper, places = span_table(key)
    return places


def draw_span_bounds(key, part):
    lower, upper, places = span_table(key)
    return jnp.stack([lower, upper], axis=1).astype(jnp.int32)


def draw_queries(key, part):
    base_key = jax.random.fold_in(key, 303)
    key_normal = jax.random.fold_in(base_key, 0)
    table = jax.random.truncated_normal(key_normal, -6.0, 6.0, (TEXT, H * HD), jnp.float32)
    return table.astype(jnp.bfloat16)


def block_scale(own_key, extent, pieces, least, high):
    loudness, own = 1.0, jax.random.fold_in(own_key, 6)
    for position, parts in pieces:
        draws = jnp.exp(jax.random.uniform(jax.random.fold_in(own, position), (parts,), jnp.float32, least / len(pieces), high / len(pieces)))
        loudness = loudness * jnp.repeat(draws, extent[position] // parts).reshape([-1 if axis == position else 1 for axis in range(len(extent))])
    return loudness


def scatter_about(stream_key, dims, width, bound, pieces=(), kind=jnp.bfloat16):
    values = width * jax.random.normal(stream_key, dims, jnp.float32)
    if pieces:
        values = values * block_scale(stream_key, dims, pieces, -0.22, 0.18)
    return jnp.clip(values, -bound, bound).astype(kind)


def setup_inputs(seed: int = 0) -> dict:
    key_list = jax.random.split(jax.random.key(seed), 7)
    return {
        "queries": draw_queries(jax.random.fold_in(key_list[6], 71), 0),
        "video_keys": draw_video_keys(jax.random.fold_in(key_list[6], 71), 0),
        "video_values": scatter_about(key_list[2], (VTOK, G * HD), 1.0, 6.0, ((0, 2),)),
        "grad_out": scatter_about(key_list[3], (TEXT, H * HD), 1.0, 6.0, ((0, 16),)),
        "positions": draw_positions(jax.random.fold_in(key_list[6], 71), 0),
        "span_bounds": draw_span_bounds(jax.random.fold_in(key_list[6], 71), 0),
    }


masked_floor = -1.0e30


def hold_low(values):
    return lax.optimization_barrier(values.astype(jnp.bfloat16)).astype(jnp.float32)


def reference(queries, video_keys, video_values, grad_out, positions, span_bounds):
    score_scale = HD ** -0.5
    per_group = H // G
    columns = jnp.arange(VTOK, dtype=jnp.int32)
    keys_all = video_keys.astype(jnp.float32)
    values_all = video_values.astype(jnp.float32)
    block_count = TEXT // TBLK
    query_blocks = queries.reshape(block_count, TBLK, H * HD)
    grad_blocks = grad_out.reshape(block_count, TBLK, H * HD)
    position_blocks = positions.reshape(block_count, TBLK)

    def one_block(carry, items):
        key_total, value_total = carry
        query_rows, grad_rows, row_positions, bounds = items
        visible = (columns[None, :] >= bounds[0]) & (columns[None, :] < bounds[1]) & (columns[None, :] <= row_positions[:, None])
        vis_heads = visible[:, None, :]
        vis_blocks = vis_heads.reshape(TBLK, 1, N_VIDEO, VID_DEV)
        outs_att, outs_dq, outs_dk, outs_dv = [], [], [], []
        for group in range(G):
            head_start = group * per_group * HD
            head_stop = (group + 1) * per_group * HD
            query_grp = query_rows[:, head_start:head_stop].astype(jnp.float32).reshape(TBLK, per_group, HD)
            grad_grp = grad_rows[:, head_start:head_stop].astype(jnp.float32).reshape(TBLK, per_group, HD)
            key_grp = keys_all[:, group * HD:(group + 1) * HD]
            value_grp = values_all[:, group * HD:(group + 1) * HD]
            scores = jnp.einsum("rhd,cd->rhc", query_grp, key_grp) * score_scale
            masked = jnp.where(vis_heads, scores, masked_floor)
            masked_blocks = masked.reshape(TBLK, per_group, N_VIDEO, VID_DEV)
            block_peak = jnp.max(masked_blocks, axis=3)
            weights = jnp.where(vis_blocks, jnp.exp(masked_blocks - block_peak[..., None]), 0.0)
            block_total = jnp.sum(weights, axis=3)
            block_out = jnp.einsum("rhnc,ncd->rhnd", hold_low(weights), value_grp.reshape(N_VIDEO, VID_DEV, HD))
            row_peak = jnp.max(block_peak, axis=2)
            factor = jnp.exp(block_peak - row_peak[..., None])
            row_total = jnp.sum(block_total * factor, axis=2)
            numer = jnp.sum(block_out * factor[..., None], axis=2)
            attended = (numer / row_total[..., None]).astype(jnp.bfloat16)
            log_norm = row_peak + jnp.log(row_total)
            delta = jnp.sum(grad_grp * lax.optimization_barrier(attended).astype(jnp.float32), axis=2)
            prob = jnp.where(vis_heads, jnp.exp(masked - log_norm[..., None]), 0.0)
            dprob = jnp.einsum("rhd,cd->rhc", grad_grp, value_grp)
            dscore = hold_low(prob * (dprob - delta[..., None]))
            outs_att.append(attended.reshape(TBLK, per_group * HD))
            outs_dq.append(jnp.einsum("rhc,cd->rhd", dscore, key_grp).reshape(TBLK, per_group * HD) * score_scale)
            outs_dk.append(jnp.einsum("rhc,rhd->cd", dscore, query_grp) * score_scale)
            outs_dv.append(jnp.einsum("rhc,rhd->cd", hold_low(prob), grad_grp))
        key_total = key_total + jnp.concatenate(outs_dk, axis=1)
        value_total = value_total + jnp.concatenate(outs_dv, axis=1)
        att_rows = jnp.concatenate(outs_att, axis=1)
        dq_rows = jnp.concatenate(outs_dq, axis=1).astype(jnp.bfloat16)
        return (key_total, value_total), (att_rows, dq_rows)

    zeros = jnp.zeros((VTOK, G * HD), jnp.float32)
    (key_total, value_total), (att_blocks, dq_blocks) = lax.scan(one_block, (zeros, zeros), (query_blocks, grad_blocks, position_blocks, span_bounds))
    return (att_blocks.reshape(TEXT, H * HD), dq_blocks.reshape(TEXT, H * HD), key_total.astype(jnp.bfloat16), value_total.astype(jnp.bfloat16))
```

```python
import functools
import math

import jax
import jax.numpy as jnp
from jax import lax
from jax.experimental import pallas as pl
from jax.experimental.pallas import tpu as pltpu
from jax.sharding import PartitionSpec as P

H = 32
G = 4
HD = 128
PER_GROUP = H // G
CORES = 2
DEPTH = 4
FLOOR = -1e30
MESH = pl.DeviceIdType.MESH
NT = (((1,), (1,)), ((), ()))


def remote(src, dst, send, recv, text, video):
    return pltpu.make_async_remote_copy(
        src_ref=src,
        dst_ref=dst,
        send_sem=send,
        recv_sem=recv,
        device_id=(text, video),
        device_id_type=MESH,
    )


def kernel(
    T, V, q_ref, go_ref, k_ref, v_ref, pos_ref, span_ref,
    att_ref, dq_ref, dk_ref, dv_ref,
    q_s, go_s, kv_s, kv_out, kv_in, k_all, v_all, bias, p_all, ds_all,
    part, r_core, s_y, r_y, s_z, r_z, s_x, r_x, att_s, dq_s,
    load_sem, out_sem, kv_send, kv_recv, fw_send, fw_recv,
    c_send, c_recv, y_send, y_recv, z_send, z_recv, x_send, x_recv,
):
    Z = DEPTH
    Y = T // (CORES * Z)
    heads = H // V
    groups = max(1, heads // PER_GROUP)
    gheads = heads // groups
    own = kv_s.shape[1]
    half = own // CORES
    gw = groups * HD
    tokens = own * V
    R = own // T
    scale = HD ** -0.5

    t = lax.axis_index("text")
    v = lax.axis_index("video")
    c = lax.rem(t, CORES)
    y = lax.rem(t // CORES, Y)
    z = t // (CORES * Y)
    sib = t + 1 - 2 * c

    def text_at(zz, yy):
        return (zz * Y + yy) * CORES + c

    def key_column(rank):
        return pl.multiple_of(((rank * heads) // PER_GROUP) * HD, HD)

    loads = [
        pltpu.make_async_copy(k_ref, kv_s.at[0], load_sem.at[0]),
        pltpu.make_async_copy(v_ref, kv_s.at[1], load_sem.at[1]),
    ]
    for gi in range(groups):
        cols = pl.ds(pl.multiple_of((v * heads + gi * gheads) * HD, HD), gheads * HD)
        loads.append(pltpu.make_async_copy(q_ref.at[:, cols], q_s.at[gi], load_sem.at[2 + 2 * gi]))
        loads.append(pltpu.make_async_copy(go_ref.at[:, cols], go_s.at[gi], load_sem.at[3 + 2 * gi]))
    for load in loads:
        load.start()

    barrier = pltpu.get_barrier_semaphore()
    partners = [(sib, v)]
    partners += [(t, lax.rem(v + k, V)) for k in range(1, V)]
    partners += [(text_at(z, lax.rem(y + k, Y)), v) for k in range(1, Y)]
    partners += [(text_at(lax.rem(z + k, Z), y), v) for k in range(1, Z)]
    for partner in partners:
        pl.semaphore_signal(barrier, inc=1, device_id=partner, device_id_type=MESH)

    loads[0].wait()
    loads[1].wait()
    rows = pl.ds(pl.multiple_of(c * half, half), half)
    for k in range(1, V):
        cols = pl.ds(key_column(lax.rem(v + k, V)), gw)
        for i in range(2):
            kv_out[k - 1, i] = kv_s[i, rows, cols].astype(jnp.float32)
    pl.semaphore_wait(barrier, len(partners))
    sends = []
    for k in range(1, V):
        copy = remote(kv_out.at[k - 1], kv_in.at[v, c], kv_send.at[k - 1], kv_recv.at[k - 1], t, lax.rem(v + k, V))
        copy.start()
        sends.append(copy)

    pos = pos_ref[...]
    low = span_ref[0, 0]
    high = span_ref[0, 1]
    token = lax.broadcasted_iota(jnp.int32, (tokens, HD), 0)
    bias[...] = jnp.where((token >= low) & (token < high) & (token <= pos), 0.0, FLOOR)
    mine = pl.ds(pl.multiple_of(v * own, own), own)
    cols = pl.ds(key_column(v), gw)
    k_all[mine, :] = kv_s[0, :, cols].astype(jnp.float32)
    v_all[mine, :] = kv_s[1, :, cols].astype(jnp.float32)

    forwards = []
    for k in range(1, V):
        source = lax.rem(v - k + V, V)
        sends[k - 1].wait_recv()
        copy = remote(kv_in.at[source, c], kv_in.at[source, c], fw_send.at[k - 1], fw_recv.at[k - 1], sib, v)
        copy.start()
        forwards.append(copy)
        there = pl.ds(pl.multiple_of(source * own + c * half, half), half)
        k_all[there, :] = kv_in[source, c, 0]
        v_all[there, :] = kv_in[source, c, 1]
    for k in range(1, V):
        source = lax.rem(v - k + V, V)
        forwards[k - 1].wait_recv()
        there = pl.ds(pl.multiple_of(source * own + (1 - c) * half, half), half)
        k_all[there, :] = kv_in[source, 1 - c, 0]
        v_all[there, :] = kv_in[source, 1 - c, 1]
    for load in loads[2:]:
        load.wait()

    pending = list(sends) + list(forwards)
    running = {}

    def start_core(gi):
        copy = remote(part.at[gi, 1 - c], r_core.at[gi], c_send.at[gi], c_recv.at[gi], sib, v)
        copy.start()
        running[gi] = [copy]

    def start_y(gi):
        running[gi][0].wait_recv()
        pending.extend(running[gi])
        s_y[gi] = part[gi, c] + r_core[gi]
        running[gi] = []
        for k in range(1, Y):
            yy = lax.rem(y + k, Y)
            copy = remote(s_y.at[gi, yy], r_y.at[gi, k - 1], y_send.at[gi, k - 1], y_recv.at[gi, k - 1], text_at(z, yy), v)
            copy.start()
            running[gi].append(copy)

    def start_z(gi):
        total = s_y[gi, y]
        for k in range(1, Y):
            running[gi][k - 1].wait_recv()
            total += r_y[gi, k - 1]
        pending.extend(running[gi])
        s_z[gi] = total
        running[gi] = []
        for k in range(1, Z):
            zz = lax.rem(z + k, Z)
            copy = remote(s_z.at[gi, zz], r_z.at[gi, k - 1], z_send.at[gi, k - 1], z_recv.at[gi, k - 1], text_at(zz, y), v)
            copy.start()
            running[gi].append(copy)

    def start_x(gi):
        total = s_z[gi, z]
        for k in range(1, Z):
            running[gi][k - 1].wait_recv()
            total += r_z[gi, k - 1]
        pending.extend(running[gi])
        s_x[gi] = total
        running[gi] = []
        for k in range(1, V):
            vv = lax.rem(v + k, V)
            copy = remote(s_x.at[gi, vv], r_x.at[gi, v], x_send.at[gi, k - 1], x_recv.at[gi, k - 1], t, vv)
            copy.start()
            running[gi].append(copy)
        r_x[gi, v] = s_x[gi, v]

    outs = []
    bias_pair = jnp.concatenate([bias[...]] * 2, axis=1)
    for gi in range(groups):
        kf = k_all[:, gi * HD : (gi + 1) * HD]
        vf = v_all[:, gi * HD : (gi + 1) * HD]
        kb = kf.astype(jnp.bfloat16)
        vb = vf.astype(jnp.bfloat16)
        kt = kf.T.astype(jnp.bfloat16)
        vt = vf.T.astype(jnp.bfloat16)
        for pair in range(gheads // 2):
            heads_here = (2 * pair, 2 * pair + 1)
            qp = jnp.concatenate([q_s[gi, :, h * HD : (h + 1) * HD] for h in heads_here], axis=0)
            gp = jnp.concatenate([go_s[gi, :, h * HD : (h + 1) * HD] for h in heads_here], axis=0)
            s = lax.dot_general(kb, qp, NT, preferred_element_type=jnp.float32)
            s = s * (scale * math.log2(math.e)) + bias_pair
            e = jnp.exp2(s - jnp.max(s, axis=0, keepdims=True))
            prob = e * (1.0 / jnp.sum(e, axis=0, keepdims=True))
            low_prob = prob.astype(jnp.bfloat16)
            dprob = lax.dot_general(vb, gp, NT, preferred_element_type=jnp.float32)
            delta = jnp.sum(prob * dprob, axis=0, keepdims=True)
            dscore = (prob * (dprob - delta)).astype(jnp.bfloat16)
            there = slice(pair * 2 * HD, (pair + 1) * 2 * HD)
            p_all[gi, :, there] = low_prob
            ds_all[gi, :, there] = dscore
            out = jnp.dot(vt, low_prob, preferred_element_type=jnp.float32).T.astype(jnp.bfloat16)
            dq = (jnp.dot(kt, dscore, preferred_element_type=jnp.float32) * scale).T.astype(jnp.bfloat16)
            for i, h in enumerate(heads_here):
                att_s[gi, :, h * HD : (h + 1) * HD] = out[i * HD : (i + 1) * HD]
                dq_s[gi, :, h * HD : (h + 1) * HD] = dq[i * HD : (i + 1) * HD]
            if gi > 0 and pair == 0:
                start_y(gi - 1)
            if gi > 0 and pair == gheads // 2 - 1:
                start_z(gi - 1)
        cols = slice(gi * gheads * HD, (gi + 1) * gheads * HD)
        for i, (src, dst) in enumerate(((att_s, att_ref), (dq_s, dq_ref))):
            copy = pltpu.make_async_copy(src.at[gi], dst.at[:, cols], out_sem.at[gi, i])
            copy.start()
            outs.append(copy)
        qg = jnp.concatenate([q_s[gi, :, h * HD : (h + 1) * HD] for h in range(gheads)], axis=0)
        gg = jnp.concatenate([go_s[gi, :, h * HD : (h + 1) * HD] for h in range(gheads)], axis=0)
        dk = jnp.dot(ds_all[gi], qg, preferred_element_type=jnp.float32) * scale
        dv = jnp.dot(p_all[gi], gg, preferred_element_type=jnp.float32)
        for i, grad in enumerate((dk, dv)):
            for vv in range(V):
                for zz in range(Z):
                    for yy in range(Y):
                        for cc in range(CORES):
                            at = (((vv * Z + zz) * Y + yy) * CORES + cc) * R
                            part[gi, cc, yy, zz, vv, i] = grad[at : at + R]
        start_core(gi)

    last = groups - 1
    if groups > 1:
        start_y(last)
        for gi in range(groups - 1):
            start_x(gi)
        start_z(last)
        start_x(last)
    else:
        start_y(last)
        start_z(last)
        start_x(last)
    for gi in range(groups):
        for copy in running[gi]:
            copy.wait_recv()
        pending.extend(running[gi])
    for g in range(G):
        if V <= G:
            found = [(g % groups, g // groups)]
        else:
            share = V // G
            found = [(0, g * share + i) for i in range(share)]
        total = sum(r_x[gi, rank] for gi, rank in found)
        dk_ref[:, g * HD : (g + 1) * HD] = total[0].astype(jnp.bfloat16)
        dv_ref[:, g * HD : (g + 1) * HD] = total[1].astype(jnp.bfloat16)
    for copy in pending:
        copy.wait_send()
    for copy in outs:
        copy.wait()


def local(T, V, queries, video_keys, video_values, grad_out, positions, span_bounds):
    Z = DEPTH
    Y = T // (CORES * Z)
    rows = queries.shape[0]
    own = video_keys.shape[0]
    tokens = own * V
    heads = H // V
    groups = max(1, heads // PER_GROUP)
    gheads = heads // groups
    gw = groups * HD
    R = own // T
    f32, bf16 = jnp.float32, jnp.bfloat16
    dma = pltpu.SemaphoreType.DMA
    hbm = pl.BlockSpec(memory_space=pl.ANY)
    vmem = pl.BlockSpec(memory_space=pltpu.VMEM)
    smem = pl.BlockSpec(memory_space=pltpu.SMEM)
    scratch = [
        pltpu.VMEM((groups, rows, gheads * HD), bf16),
        pltpu.VMEM((groups, rows, gheads * HD), bf16),
        pltpu.VMEM((2, own, G * HD), bf16),
        pltpu.VMEM((V - 1, 2, own // CORES, gw), f32),
        pltpu.VMEM((V, CORES, 2, own // CORES, gw), f32),
        pltpu.VMEM((tokens, gw), f32),
        pltpu.VMEM((tokens, gw), f32),
        pltpu.VMEM((tokens, rows), f32),
        pltpu.VMEM((groups, tokens, gheads * rows), bf16),
        pltpu.VMEM((groups, tokens, gheads * rows), bf16),
        pltpu.VMEM((groups, CORES, Y, Z, V, 2, R, HD), f32),
        pltpu.VMEM((groups, Y, Z, V, 2, R, HD), f32),
        pltpu.VMEM((groups, Y, Z, V, 2, R, HD), f32),
        pltpu.VMEM((groups, Y - 1, Z, V, 2, R, HD), f32),
        pltpu.VMEM((groups, Z, V, 2, R, HD), f32),
        pltpu.VMEM((groups, Z - 1, V, 2, R, HD), f32),
        pltpu.VMEM((groups, V, 2, R, HD), f32),
        pltpu.VMEM((groups, V, 2, R, HD), f32),
        pltpu.VMEM((groups, rows, gheads * HD), bf16),
        pltpu.VMEM((groups, rows, gheads * HD), bf16),
        dma((2 + 2 * groups,)),
        dma((groups, 2)),
        dma((V - 1,)), dma((V - 1,)), dma((V - 1,)), dma((V - 1,)),
        dma((groups,)), dma((groups,)),
        dma((groups, Y - 1)), dma((groups, Y - 1)),
        dma((groups, Z - 1)), dma((groups, Z - 1)),
        dma((groups, V - 1)), dma((groups, V - 1)),
    ]
    return pl.pallas_call(
        functools.partial(kernel, T, V),
        out_shape=(
            jax.ShapeDtypeStruct((rows, heads * HD), bf16),
            jax.ShapeDtypeStruct((rows, heads * HD), bf16),
            jax.ShapeDtypeStruct((R, G * HD), bf16),
            jax.ShapeDtypeStruct((R, G * HD), bf16),
        ),
        in_specs=[hbm, hbm, hbm, hbm, vmem, smem],
        out_specs=(hbm, hbm, vmem, vmem),
        scratch_shapes=scratch,
        compiler_params=pltpu.CompilerParams(
            collective_id=0, has_side_effects=True, vmem_limit_bytes=56 * 1024 * 1024
        ),
        cost_estimate=pl.CostEstimate(
            flops=12 * rows * heads * tokens * HD,
            bytes_accessed=8 * rows * heads * HD + 4 * own * G * HD,
            transcendentals=rows * heads * tokens,
        ),
        name="attention",
    )(queries, grad_out, video_keys, video_values, positions.reshape(1, rows), span_bounds)


def solution(mesh):
    placed = (
        P("text", None),
        P("video", None),
        P("video", None),
        P("text", None),
        P("text"),
        P("text", None),
    )
    return jax.shard_map(
        functools.partial(local, mesh.shape["text"], mesh.shape["video"]),
        mesh=mesh,
        in_specs=placed,
        out_specs=(
            P("text", "video"),
            P("text", "video"),
            P(("video", "text"), None),
            P(("video", "text"), None),
        ),
        check_vma=False,
    )
```

```python
import functools
import math

import jax
import jax.numpy as jnp
from jax import lax
from jax.experimental import pallas as pl
from jax.experimental.pallas import tpu as pltpu
from jax.sharding import PartitionSpec as P

H = 32
G = 4
HD = 128
PER_GROUP = H // G
CORES = 2
DEPTH = 4
FLOOR = -1e30
MESH = pl.DeviceIdType.MESH
NT = (((1,), (1,)), ((), ()))


def remote(src, dst, send, recv, text, video):
    return pltpu.make_async_remote_copy(
        src_ref=src,
        dst_ref=dst,
        send_sem=send,
        recv_sem=recv,
        device_id=(text, video),
        device_id_type=MESH,
    )


def kernel(
    T, V, q_ref, go_ref, k_ref, v_ref, pos_ref, span_ref,
    att_ref, dq_ref, dk_ref, dv_ref,
    q_s, go_s, kv_s, kv_out, kv_in, kv_all, bias, s_all, dp_own, p_all, ds_all,
    part, r_core, s_y, r_y, s_z, r_z, s_x, r_x, att_s, dq_s,
    load_sem, out_sem, kv_send, kv_recv, fw_send, fw_recv,
    c_send, c_recv, y_send, y_recv, z_send, z_recv, x_send, x_recv,
):
    Z = DEPTH
    Y = T // (CORES * Z)
    heads = H // V
    groups = max(1, heads // PER_GROUP)
    gheads = heads // groups
    own = kv_s.shape[1]
    half = own // CORES
    gw = groups * HD
    R = own // T
    scale = HD ** -0.5
    f32, bf16 = jnp.float32, jnp.bfloat16

    t = lax.axis_index("text")
    v = lax.axis_index("video")
    c = lax.rem(t, CORES)
    y = lax.rem(t // CORES, Y)
    z = t // (CORES * Y)
    sib = t + 1 - 2 * c

    def text_at(zz, yy):
        return (zz * Y + yy) * CORES + c

    def key_column(rank):
        return pl.multiple_of(((rank * heads) // PER_GROUP) * HD, HD)

    def source(k):
        return lax.rem(v - k + V, V)

    loads = [
        pltpu.make_async_copy(k_ref, kv_s.at[0], load_sem.at[0]),
        pltpu.make_async_copy(v_ref, kv_s.at[1], load_sem.at[1]),
    ]
    for gi in range(groups):
        cols = pl.ds(pl.multiple_of((v * heads + gi * gheads) * HD, HD), gheads * HD)
        loads.append(pltpu.make_async_copy(q_ref.at[:, cols], q_s.at[gi], load_sem.at[2 + 2 * gi]))
        loads.append(pltpu.make_async_copy(go_ref.at[:, cols], go_s.at[gi], load_sem.at[3 + 2 * gi]))
    for load in loads:
        load.start()

    barrier = pltpu.get_barrier_semaphore()
    partners = [(sib, v)]
    partners += [(t, lax.rem(v + k, V)) for k in range(1, V)]
    partners += [(text_at(z, lax.rem(y + k, Y)), v) for k in range(1, Y)]
    partners += [(text_at(lax.rem(z + k, Z), y), v) for k in range(1, Z)]
    for partner in partners:
        pl.semaphore_signal(barrier, inc=1, device_id=partner, device_id_type=MESH)

    loads[0].wait()
    loads[1].wait()
    rows = pl.ds(pl.multiple_of(c * half, half), half)
    rest = pl.ds(pl.multiple_of((1 - c) * half, half), half)
    for k in range(1, V):
        cols = pl.ds(key_column(lax.rem(v + k, V)), gw)
        for i in range(2):
            kv_out[i, k - 1] = kv_s[i, rows, cols].astype(f32)
    pl.semaphore_wait(barrier, len(partners))
    sends = [[], []]
    for i in range(2):
        for k in range(1, V):
            copy = remote(
                kv_out.at[i, k - 1], kv_in.at[i, k - 1, c], kv_send.at[i, k - 1], kv_recv.at[i, k - 1], t, lax.rem(v + k, V)
            )
            copy.start()
            sends[i].append(copy)
    forwards = [[], []]

    def forward(i):
        for k in range(1, V):
            sends[i][k - 1].wait_recv()
            copy = remote(
                kv_in.at[i, k - 1, c], kv_in.at[i, k - 1, c], fw_send.at[i, k - 1], fw_recv.at[i, k - 1], sib, v
            )
            copy.start()
            forwards[i].append(copy)
            kv_all[i, k, rows, :] = kv_in[i, k - 1, c]

    def collect(i):
        for k in range(1, V):
            forwards[i][k - 1].wait_recv()
            kv_all[i, k, rest, :] = kv_in[i, k - 1, 1 - c]

    pending = []
    flying = []

    def start_core(p):
        copy = remote(part.at[p, 1 - c], r_core.at[p], c_send.at[p], c_recv.at[p], sib, v)
        copy.start()
        return [copy]

    def start_y(p, before):
        before[0].wait_recv()
        s_y[p] = part[p, c] + r_core[p]
        copies = []
        for k in range(1, Y):
            yy = lax.rem(y + k, Y)
            copy = remote(s_y.at[p, yy], r_y.at[p, k - 1], y_send.at[p, k - 1], y_recv.at[p, k - 1], text_at(z, yy), v)
            copy.start()
            copies.append(copy)
        return copies

    def start_z(p, before):
        total = s_y[p, y]
        for k in range(1, Y):
            before[k - 1].wait_recv()
            total += r_y[p, k - 1]
        s_z[p] = total
        copies = []
        for k in range(1, Z):
            zz = lax.rem(z + k, Z)
            copy = remote(s_z.at[p, zz], r_z.at[p, k - 1], z_send.at[p, k - 1], z_recv.at[p, k - 1], text_at(zz, y), v)
            copy.start()
            copies.append(copy)
        return copies

    def start_x(p, before):
        total = s_z[p, z]
        for k in range(1, Z):
            before[k - 1].wait_recv()
            total += r_z[p, k - 1]
        s_x[p] = total
        copies = []
        for k in range(1, V):
            vv = lax.rem(v + k, V)
            copy = remote(s_x.at[p, vv], r_x.at[p, v], x_send.at[p, k - 1], x_recv.at[p, k - 1], t, vv)
            copy.start()
            copies.append(copy)
        r_x[p, v] = s_x[p, v]
        return copies

    stages = (start_y, start_z, start_x)

    def launch(p, grad):
        for j in range(V):
            for zz in range(Z):
                for yy in range(Y):
                    for cc in range(CORES):
                        at = j * own + ((zz * Y + yy) * CORES + cc) * R
                        part[p, cc, yy, zz, source(j)] = grad[at : at + R]
        flying.append([p, 0, start_core(p)])

    def tick():
        for piece in reversed(flying):
            p, stage, copies = piece
            if stage < len(stages):
                pending.extend(copies)
                piece[2] = stages[stage](p, copies)
                piece[1] = stage + 1

    pos = pos_ref[...]
    low = span_ref[0, 0]
    high = span_ref[0, 1]
    for j in range(V):
        token = source(j) * own + lax.broadcasted_iota(jnp.int32, (own, HD), 0)
        bias[j] = jnp.where((token >= low) & (token < high) & (token <= pos), 0.0, FLOOR)
    cols = pl.ds(key_column(v), gw)
    for i in range(2):
        kv_all[i, 0] = kv_s[i, :, cols].astype(f32)
    for load in loads[2:]:
        load.wait()

    pairs = gheads // 2

    def head_rows(ref, gi, first, count):
        return jnp.concatenate([ref[gi, :, h * HD : (h + 1) * HD] for h in range(first, first + count)], axis=0)

    def key_rows(i, gi, j):
        return kv_all[i, j, :, gi * HD : (gi + 1) * HD].astype(bf16)

    def scores(keys, queries, j):
        raw = lax.dot_general(keys, queries, NT, preferred_element_type=f32)
        return raw * (scale * math.log2(math.e)) + jnp.concatenate([bias[j]] * 2, axis=1)

    for gi in range(groups):
        keys = key_rows(0, gi, 0)
        values = key_rows(1, gi, 0)
        for pair in range(pairs):
            there = slice(pair * 2 * HD, (pair + 1) * 2 * HD)
            s_all[gi, 0, :, there] = scores(keys, head_rows(q_s, gi, 2 * pair, 2), 0)
            dp_own[gi, :, there] = lax.dot_general(
                values, head_rows(go_s, gi, 2 * pair, 2), NT, preferred_element_type=f32
            )

    forward(0)
    collect(0)
    for gi in range(groups):
        keys = [key_rows(0, gi, j) for j in range(V)]
        for pair in range(pairs):
            there = slice(pair * 2 * HD, (pair + 1) * 2 * HD)
            queries = head_rows(q_s, gi, 2 * pair, 2)
            s = [s_all[gi, 0, :, there]] + [scores(keys[j], queries, j) for j in range(1, V)]
            peak = functools.reduce(jnp.maximum, [jnp.max(x, axis=0, keepdims=True) for x in s])
            e = [jnp.exp2(x - peak) for x in s]
            inverse = 1.0 / sum(jnp.sum(x, axis=0, keepdims=True) for x in e)
            for j in range(V):
                prob = e[j] * inverse
                s_all[gi, j, :, there] = prob
                p_all[gi, j * own : (j + 1) * own, there] = prob.astype(bf16)
            if gi > 0 and pair == pairs // 2 - 1:
                tick()
        grad = jnp.dot(p_all[gi], head_rows(go_s, gi, 0, gheads), preferred_element_type=f32)
        launch(gi, grad)
        if gi == 0:
            forward(1)

    collect(1)
    outs = []
    for gi in range(groups):
        kt = jnp.concatenate([kv_all[0, j, :, gi * HD : (gi + 1) * HD].T for j in range(V)], axis=1).astype(bf16)
        vt = jnp.concatenate([kv_all[1, j, :, gi * HD : (gi + 1) * HD].T for j in range(V)], axis=1).astype(bf16)
        values = [key_rows(1, gi, j) for j in range(V)]
        for pair in range(pairs):
            there = slice(pair * 2 * HD, (pair + 1) * 2 * HD)
            gp = head_rows(go_s, gi, 2 * pair, 2)
            dprob = [dp_own[gi, :, there]] + [
                lax.dot_general(values[j], gp, NT, preferred_element_type=f32) for j in range(1, V)
            ]
            prob = [s_all[gi, j, :, there] for j in range(V)]
            delta = sum(jnp.sum(prob[j] * dprob[j], axis=0, keepdims=True) for j in range(V))
            for j in range(V):
                ds_all[gi, j * own : (j + 1) * own, there] = (prob[j] * (dprob[j] - delta)).astype(bf16)
            out = jnp.dot(vt, p_all[gi, :, there], preferred_element_type=f32).T.astype(bf16)
            dq = (jnp.dot(kt, ds_all[gi, :, there], preferred_element_type=f32) * scale).T.astype(bf16)
            for i in range(2):
                h = 2 * pair + i
                att_s[gi, :, h * HD : (h + 1) * HD] = out[i * HD : (i + 1) * HD]
                dq_s[gi, :, h * HD : (h + 1) * HD] = dq[i * HD : (i + 1) * HD]
            if pair == pairs // 2 - 1:
                tick()
        grad = jnp.dot(ds_all[gi], head_rows(q_s, gi, 0, gheads), preferred_element_type=f32) * scale
        launch(groups + gi, grad)
        cols = slice(gi * gheads * HD, (gi + 1) * gheads * HD)
        for i, (src, dst) in enumerate(((att_s, att_ref), (dq_s, dq_ref))):
            copy = pltpu.make_async_copy(src.at[gi], dst.at[:, cols], out_sem.at[gi, i])
            copy.start()
            outs.append(copy)

    for _ in stages:
        tick()
    for _, _, copies in flying:
        for copy in copies:
            copy.wait_recv()
        pending.extend(copies)
    for g in range(G):
        if V <= G:
            found = [(g % groups, g // groups)]
        else:
            share = V // G
            found = [(0, g * share + i) for i in range(share)]
        there = slice(g * HD, (g + 1) * HD)
        dv_ref[:, there] = sum(r_x[gi, rank] for gi, rank in found).astype(bf16)
        dk_ref[:, there] = sum(r_x[groups + gi, rank] for gi, rank in found).astype(bf16)
    for copy in pending + sends[0] + sends[1] + forwards[0] + forwards[1]:
        copy.wait_send()
    for copy in outs:
        copy.wait()


def hand_on(*refs):
    count = (len(refs) - 1) // 2
    sems = refs[-1]
    copies = [pltpu.make_async_copy(refs[i], refs[count + i], sems.at[i]) for i in range(count)]
    for copy in copies:
        copy.start()
    for copy in copies:
        copy.wait()


def local(T, V, queries, video_keys, video_values, grad_out, positions, span_bounds):
    Z = DEPTH
    Y = T // (CORES * Z)
    rows = queries.shape[0]
    own = video_keys.shape[0]
    tokens = own * V
    heads = H // V
    groups = max(1, heads // PER_GROUP)
    gheads = heads // groups
    gw = groups * HD
    R = own // T
    f32, bf16 = jnp.float32, jnp.bfloat16
    dma = pltpu.SemaphoreType.DMA
    hbm = pl.BlockSpec(memory_space=pl.ANY)
    vmem = pl.BlockSpec(memory_space=pltpu.VMEM)
    smem = pl.BlockSpec(memory_space=pltpu.SMEM)
    pieces = 2 * groups
    scratch = [
        pltpu.VMEM((groups, rows, gheads * HD), bf16),
        pltpu.VMEM((groups, rows, gheads * HD), bf16),
        pltpu.VMEM((2, own, G * HD), bf16),
        pltpu.VMEM((2, V - 1, own // CORES, gw), f32),
        pltpu.VMEM((2, V - 1, CORES, own // CORES, gw), f32),
        pltpu.VMEM((2, V, own, gw), f32),
        pltpu.VMEM((V, own, rows), f32),
        pltpu.VMEM((groups, V, own, gheads * rows), f32),
        pltpu.VMEM((groups, own, gheads * rows), f32),
        pltpu.VMEM((groups, tokens, gheads * rows), bf16),
        pltpu.VMEM((groups, tokens, gheads * rows), bf16),
        pltpu.VMEM((pieces, CORES, Y, Z, V, R, HD), f32),
        pltpu.VMEM((pieces, Y, Z, V, R, HD), f32),
        pltpu.VMEM((pieces, Y, Z, V, R, HD), f32),
        pltpu.VMEM((pieces, Y - 1, Z, V, R, HD), f32),
        pltpu.VMEM((pieces, Z, V, R, HD), f32),
        pltpu.VMEM((pieces, Z - 1, V, R, HD), f32),
        pltpu.VMEM((pieces, V, R, HD), f32),
        pltpu.VMEM((pieces, V, R, HD), f32),
        pltpu.VMEM((groups, rows, gheads * HD), bf16),
        pltpu.VMEM((groups, rows, gheads * HD), bf16),
        dma((2 + 2 * groups,)),
        dma((groups, 2)),
        dma((2, V - 1)), dma((2, V - 1)), dma((2, V - 1)), dma((2, V - 1)),
        dma((pieces,)), dma((pieces,)),
        dma((pieces, Y - 1)), dma((pieces, Y - 1)),
        dma((pieces, Z - 1)), dma((pieces, Z - 1)),
        dma((pieces, V - 1)), dma((pieces, V - 1)),
    ]
    shapes = (
        jax.ShapeDtypeStruct((rows, heads * HD), bf16),
        jax.ShapeDtypeStruct((rows, heads * HD), bf16),
        jax.ShapeDtypeStruct((R, G * HD), bf16),
        jax.ShapeDtypeStruct((R, G * HD), bf16),
    )
    results = pl.pallas_call(
        functools.partial(kernel, T, V),
        out_shape=shapes,
        in_specs=[hbm, hbm, hbm, hbm, vmem, smem],
        out_specs=(hbm, hbm, vmem, vmem),
        scratch_shapes=scratch,
        compiler_params=pltpu.CompilerParams(
            collective_id=0, has_side_effects=True, vmem_limit_bytes=56 * 1024 * 1024
        ),
        cost_estimate=pl.CostEstimate(
            flops=12 * rows * heads * tokens * HD,
            bytes_accessed=8 * rows * heads * HD + 4 * own * G * HD,
            transcendentals=rows * heads * tokens,
        ),
        name="attention",
    )(queries, grad_out, video_keys, video_values, positions.reshape(1, rows), span_bounds)
    return pl.pallas_call(
        hand_on,
        out_shape=shapes,
        in_specs=[hbm] * 4,
        out_specs=(hbm,) * 4,
        scratch_shapes=[dma((4,))],
        name="hand_on",
    )(*results)


def solution(mesh):
    placed = (
        P("text", None),
        P("video", None),
        P("video", None),
        P("text", None),
        P("text"),
        P("text", None),
    )
    return jax.shard_map(
        functools.partial(local, mesh.shape["text"], mesh.shape["video"]),
        mesh=mesh,
        in_specs=placed,
        out_specs=(
            P("text", "video"),
            P("text", "video"),
            P(("video", "text"), None),
            P(("video", "text"), None),
        ),
        check_vma=False,
    )
```

```python
import functools
import math

import jax
import jax.numpy as jnp
from jax import lax
from jax.experimental import pallas as pl
from jax.experimental.pallas import tpu as pltpu
from jax.sharding import PartitionSpec as P

H = 32
G = 4
HD = 128
PER_GROUP = H // G
CORES = 2
DEPTH = 4
FLOOR = -1e30
MESH = pl.DeviceIdType.MESH
NT = (((1,), (1,)), ((), ()))


def remote(src, dst, send, recv, text, video):
    return pltpu.make_async_remote_copy(
        src_ref=src,
        dst_ref=dst,
        send_sem=send,
        recv_sem=recv,
        device_id=(text, video),
        device_id_type=MESH,
    )


def kernel(
    T, V, q_ref, go_ref, k_ref, v_ref, pos_ref, span_ref,
    att_ref, dq_ref, dk_ref, dv_ref,
    q_s, go_s, kv_s, kv_out, kv_in, kv_all, bias, s_all, dp_own, p_all, ds_all,
    part, r_core, s_y, r_y, s_z, r_z, s_x, r_x, att_s, dq_s,
    load_sem, out_sem, kv_send, kv_recv, fw_send, fw_recv,
    c_send, c_recv, y_send, y_recv, z_send, z_recv, x_send, x_recv,
):
    Z = DEPTH
    Y = T // (CORES * Z)
    heads = H // V
    groups = max(1, heads // PER_GROUP)
    gheads = heads // groups
    own = kv_s.shape[1]
    half = own // CORES
    gw = groups * HD
    R = own // T
    scale = HD ** -0.5
    f32, bf16 = jnp.float32, jnp.bfloat16

    t = lax.axis_index("text")
    v = lax.axis_index("video")
    c = lax.rem(t, CORES)
    y = lax.rem(t // CORES, Y)
    z = t // (CORES * Y)
    sib = t + 1 - 2 * c

    def text_at(zz, yy):
        return (zz * Y + yy) * CORES + c

    def key_column(rank):
        return pl.multiple_of(((rank * heads) // PER_GROUP) * HD, HD)

    def source(k):
        return lax.rem(v - k + V, V)

    loads = [
        pltpu.make_async_copy(k_ref, kv_s.at[0], load_sem.at[0]),
        pltpu.make_async_copy(v_ref, kv_s.at[1], load_sem.at[1]),
    ]
    for gi in range(groups):
        cols = pl.ds(pl.multiple_of((v * heads + gi * gheads) * HD, HD), gheads * HD)
        loads.append(pltpu.make_async_copy(q_ref.at[:, cols], q_s.at[gi], load_sem.at[2 + 2 * gi]))
        loads.append(pltpu.make_async_copy(go_ref.at[:, cols], go_s.at[gi], load_sem.at[3 + 2 * gi]))
    for load in loads:
        load.start()

    barrier = pltpu.get_barrier_semaphore()
    partners = [(sib, v)]
    partners += [(t, lax.rem(v + k, V)) for k in range(1, V)]
    partners += [(text_at(z, lax.rem(y + k, Y)), v) for k in range(1, Y)]
    partners += [(text_at(lax.rem(z + k, Z), y), v) for k in range(1, Z)]
    for partner in partners:
        pl.semaphore_signal(barrier, inc=1, device_id=partner, device_id_type=MESH)

    loads[0].wait()
    loads[1].wait()
    rows = pl.ds(pl.multiple_of(c * half, half), half)
    rest = pl.ds(pl.multiple_of((1 - c) * half, half), half)
    for k in range(1, V):
        cols = pl.ds(key_column(lax.rem(v + k, V)), gw)
        for i in range(2):
            kv_out[i, k - 1] = kv_s[i, rows, cols].astype(f32)
    pl.semaphore_wait(barrier, len(partners))
    sends = [[], []]
    for i in range(2):
        for k in range(1, V):
            copy = remote(
                kv_out.at[i, k - 1], kv_in.at[i, k - 1, c], kv_send.at[i, k - 1], kv_recv.at[i, k - 1], t, lax.rem(v + k, V)
            )
            copy.start()
            sends[i].append(copy)
    forwards = [[], []]

    def forward(i):
        for k in range(1, V):
            sends[i][k - 1].wait_recv()
            copy = remote(
                kv_in.at[i, k - 1, c], kv_in.at[i, k - 1, c], fw_send.at[i, k - 1], fw_recv.at[i, k - 1], sib, v
            )
            copy.start()
            forwards[i].append(copy)
            kv_all[i, k, rows, :] = kv_in[i, k - 1, c]

    def collect(i):
        for k in range(1, V):
            forwards[i][k - 1].wait_recv()
            kv_all[i, k, rest, :] = kv_in[i, k - 1, 1 - c]

    pending = []
    flying = []

    def start_core(p):
        copy = remote(part.at[p, 1 - c], r_core.at[p], c_send.at[p], c_recv.at[p], sib, v)
        copy.start()
        return [copy]

    def start_y(p, before):
        before[0].wait_recv()
        s_y[p] = part[p, c] + r_core[p]
        copies = []
        for k in range(1, Y):
            yy = lax.rem(y + k, Y)
            copy = remote(s_y.at[p, yy], r_y.at[p, k - 1], y_send.at[p, k - 1], y_recv.at[p, k - 1], text_at(z, yy), v)
            copy.start()
            copies.append(copy)
        return copies

    def start_z(p, before):
        total = s_y[p, y]
        for k in range(1, Y):
            before[k - 1].wait_recv()
            total += r_y[p, k - 1]
        s_z[p] = total
        copies = []
        for k in range(1, Z):
            zz = lax.rem(z + k, Z)
            copy = remote(s_z.at[p, zz], r_z.at[p, k - 1], z_send.at[p, k - 1], z_recv.at[p, k - 1], text_at(zz, y), v)
            copy.start()
            copies.append(copy)
        return copies

    def start_x(p, before):
        total = s_z[p, z]
        for k in range(1, Z):
            before[k - 1].wait_recv()
            total += r_z[p, k - 1]
        s_x[p] = total
        copies = []
        for k in range(1, V):
            vv = lax.rem(v + k, V)
            copy = remote(s_x.at[p, vv], r_x.at[p, v], x_send.at[p, k - 1], x_recv.at[p, k - 1], t, vv)
            copy.start()
            copies.append(copy)
        r_x[p, v] = s_x[p, v]
        return copies

    stages = (start_y, start_z, start_x)

    def launch(p, grad):
        for j in range(V):
            for zz in range(Z):
                for yy in range(Y):
                    for cc in range(CORES):
                        at = j * own + ((zz * Y + yy) * CORES + cc) * R
                        part[p, cc, yy, zz, source(j)] = grad[at : at + R]
        flying.append([p, 0, start_core(p)])

    def tick():
        for piece in reversed(flying):
            p, stage, copies = piece
            if stage < len(stages):
                pending.extend(copies)
                piece[2] = stages[stage](p, copies)
                piece[1] = stage + 1

    pos = pos_ref[...]
    low = span_ref[0, 0]
    high = span_ref[0, 1]
    for j in range(V):
        token = source(j) * own + lax.broadcasted_iota(jnp.int32, (own, HD), 0)
        bias[j] = jnp.where((token >= low) & (token < high) & (token <= pos), 0.0, FLOOR)
    cols = pl.ds(key_column(v), gw)
    for i in range(2):
        kv_all[i, 0] = kv_s[i, :, cols].astype(f32)
    for load in loads[2:]:
        load.wait()

    pairs = gheads // 2

    def head_rows(ref, gi, first, count):
        return jnp.concatenate([ref[gi, :, h * HD : (h + 1) * HD] for h in range(first, first + count)], axis=0)

    def pair_columns(pair):
        return pl.ds(pl.multiple_of(pair * 2 * HD, 2 * HD), 2 * HD)

    def head_pair(ref, gi, there):
        both = ref[gi, :, there]
        return jnp.concatenate([both[:, :HD], both[:, HD:]], axis=0)

    def key_rows(i, gi, j):
        return kv_all[i, j, :, gi * HD : (gi + 1) * HD].astype(bf16)

    def scores(keys, queries, j):
        raw = lax.dot_general(keys, queries, NT, preferred_element_type=f32)
        return raw * (scale * math.log2(math.e)) + jnp.concatenate([bias[j]] * 2, axis=1)

    for gi in range(groups):
        keys = key_rows(0, gi, 0)
        values = key_rows(1, gi, 0)

        @pl.loop(0, pairs)
        def _(pair):
            there = pair_columns(pair)
            s_all[gi, 0, :, there] = scores(keys, head_pair(q_s, gi, there), 0)
            dp_own[gi, :, there] = lax.dot_general(
                values, head_pair(go_s, gi, there), NT, preferred_element_type=f32
            )

    forward(0)
    collect(0)
    for gi in range(groups):
        keys = [key_rows(0, gi, j) for j in range(V)]

        @pl.loop(0, pairs)
        def _(pair):
            there = pair_columns(pair)
            queries = head_pair(q_s, gi, there)
            s = [s_all[gi, 0, :, there]] + [scores(keys[j], queries, j) for j in range(1, V)]
            peak = functools.reduce(jnp.maximum, [jnp.max(x, axis=0, keepdims=True) for x in s])
            e = [jnp.exp2(x - peak) for x in s]
            inverse = 1.0 / sum(jnp.sum(x, axis=0, keepdims=True) for x in e)
            for j in range(V):
                prob = e[j] * inverse
                s_all[gi, j, :, there] = prob
                p_all[gi, j * own : (j + 1) * own, there] = prob.astype(bf16)

        tick()
        grad = jnp.dot(p_all[gi], head_rows(go_s, gi, 0, gheads), preferred_element_type=f32)
        launch(gi, grad)
        if gi == 0:
            forward(1)

    collect(1)
    outs = []
    for gi in range(groups):
        kt = jnp.concatenate([kv_all[0, j, :, gi * HD : (gi + 1) * HD].T for j in range(V)], axis=1).astype(bf16)
        vt = jnp.concatenate([kv_all[1, j, :, gi * HD : (gi + 1) * HD].T for j in range(V)], axis=1).astype(bf16)
        values = [key_rows(1, gi, j) for j in range(V)]

        @pl.loop(0, pairs)
        def _(pair):
            there = pair_columns(pair)
            gp = head_pair(go_s, gi, there)
            dprob = [dp_own[gi, :, there]] + [
                lax.dot_general(values[j], gp, NT, preferred_element_type=f32) for j in range(1, V)
            ]
            prob = [s_all[gi, j, :, there] for j in range(V)]
            delta = sum(jnp.sum(prob[j] * dprob[j], axis=0, keepdims=True) for j in range(V))
            for j in range(V):
                ds_all[gi, j * own : (j + 1) * own, there] = (prob[j] * (dprob[j] - delta)).astype(bf16)
            out = jnp.dot(vt, p_all[gi, :, there], preferred_element_type=f32).T.astype(bf16)
            dq = (jnp.dot(kt, ds_all[gi, :, there], preferred_element_type=f32) * scale).T.astype(bf16)
            att_s[gi, :, there] = jnp.concatenate([out[:HD], out[HD:]], axis=1)
            dq_s[gi, :, there] = jnp.concatenate([dq[:HD], dq[HD:]], axis=1)

        tick()
        grad = jnp.dot(ds_all[gi], head_rows(q_s, gi, 0, gheads), preferred_element_type=f32) * scale
        launch(groups + gi, grad)
        cols = slice(gi * gheads * HD, (gi + 1) * gheads * HD)
        for i, (src, dst) in enumerate(((att_s, att_ref), (dq_s, dq_ref))):
            copy = pltpu.make_async_copy(src.at[gi], dst.at[:, cols], out_sem.at[gi, i])
            copy.start()
            outs.append(copy)

    for _ in stages:
        tick()
    for _, _, copies in flying:
        for copy in copies:
            copy.wait_recv()
        pending.extend(copies)
    for g in range(G):
        if V <= G:
            found = [(g % groups, g // groups)]
        else:
            share = V // G
            found = [(0, g * share + i) for i in range(share)]
        there = slice(g * HD, (g + 1) * HD)
        dv_ref[:, there] = sum(r_x[gi, rank] for gi, rank in found).astype(bf16)
        dk_ref[:, there] = sum(r_x[groups + gi, rank] for gi, rank in found).astype(bf16)
    for copy in pending + sends[0] + sends[1] + forwards[0] + forwards[1]:
        copy.wait_send()
    for copy in outs:
        copy.wait()


def hand_on(*refs):
    sources, results, held, sems = refs[:4], refs[4:8], refs[8:12], refs[12]
    arrivals = [pltpu.make_async_copy(sources[i], held[i], sems.at[0, i]) for i in range(4)]
    departures = [pltpu.make_async_copy(held[i], results[i], sems.at[1, i]) for i in range(4)]
    for copy in arrivals:
        copy.start()
    for arrival, departure in zip(arrivals, departures):
        arrival.wait()
        departure.start()
    for copy in departures:
        copy.wait()


def local(T, V, queries, video_keys, video_values, grad_out, positions, span_bounds):
    Z = DEPTH
    Y = T // (CORES * Z)
    rows = queries.shape[0]
    own = video_keys.shape[0]
    tokens = own * V
    heads = H // V
    groups = max(1, heads // PER_GROUP)
    gheads = heads // groups
    gw = groups * HD
    R = own // T
    f32, bf16 = jnp.float32, jnp.bfloat16
    dma = pltpu.SemaphoreType.DMA
    hbm = pl.BlockSpec(memory_space=pl.ANY)
    vmem = pl.BlockSpec(memory_space=pltpu.VMEM)
    smem = pl.BlockSpec(memory_space=pltpu.SMEM)
    pieces = 2 * groups
    scratch = [
        pltpu.VMEM((groups, rows, gheads * HD), bf16),
        pltpu.VMEM((groups, rows, gheads * HD), bf16),
        pltpu.VMEM((2, own, G * HD), bf16),
        pltpu.VMEM((2, V - 1, own // CORES, gw), f32),
        pltpu.VMEM((2, V - 1, CORES, own // CORES, gw), f32),
        pltpu.VMEM((2, V, own, gw), f32),
        pltpu.VMEM((V, own, rows), f32),
        pltpu.VMEM((groups, V, own, gheads * rows), f32),
        pltpu.VMEM((groups, own, gheads * rows), f32),
        pltpu.VMEM((groups, tokens, gheads * rows), bf16),
        pltpu.VMEM((groups, tokens, gheads * rows), bf16),
        pltpu.VMEM((pieces, CORES, Y, Z, V, R, HD), f32),
        pltpu.VMEM((pieces, Y, Z, V, R, HD), f32),
        pltpu.VMEM((pieces, Y, Z, V, R, HD), f32),
        pltpu.VMEM((pieces, Y - 1, Z, V, R, HD), f32),
        pltpu.VMEM((pieces, Z, V, R, HD), f32),
        pltpu.VMEM((pieces, Z - 1, V, R, HD), f32),
        pltpu.VMEM((pieces, V, R, HD), f32),
        pltpu.VMEM((pieces, V, R, HD), f32),
        pltpu.VMEM((groups, rows, gheads * HD), bf16),
        pltpu.VMEM((groups, rows, gheads * HD), bf16),
        dma((2 + 2 * groups,)),
        dma((groups, 2)),
        dma((2, V - 1)), dma((2, V - 1)), dma((2, V - 1)), dma((2, V - 1)),
        dma((pieces,)), dma((pieces,)),
        dma((pieces, Y - 1)), dma((pieces, Y - 1)),
        dma((pieces, Z - 1)), dma((pieces, Z - 1)),
        dma((pieces, V - 1)), dma((pieces, V - 1)),
    ]
    shapes = (
        jax.ShapeDtypeStruct((rows, heads * HD), bf16),
        jax.ShapeDtypeStruct((rows, heads * HD), bf16),
        jax.ShapeDtypeStruct((R, G * HD), bf16),
        jax.ShapeDtypeStruct((R, G * HD), bf16),
    )
    results = pl.pallas_call(
        functools.partial(kernel, T, V),
        out_shape=shapes,
        in_specs=[hbm, hbm, hbm, hbm, vmem, smem],
        out_specs=(hbm, hbm, vmem, vmem),
        scratch_shapes=scratch,
        compiler_params=pltpu.CompilerParams(
            collective_id=0, has_side_effects=True, vmem_limit_bytes=56 * 1024 * 1024
        ),
        cost_estimate=pl.CostEstimate(
            flops=12 * rows * heads * tokens * HD,
            bytes_accessed=8 * rows * heads * HD + 4 * own * G * HD,
            transcendentals=rows * heads * tokens,
        ),
        name="attention",
    )(queries, grad_out, video_keys, video_values, positions.reshape(1, rows), span_bounds)
    return pl.pallas_call(
        hand_on,
        out_shape=shapes,
        in_specs=[hbm] * 4,
        out_specs=(hbm,) * 4,
        scratch_shapes=[pltpu.VMEM(shape.shape, bf16) for shape in shapes] + [dma((2, 4))],
        name="hand_on",
    )(*results)


def solution(mesh):
    placed = (
        P("text", None),
        P("video", None),
        P("video", None),
        P("text", None),
        P("text"),
        P("text", None),
    )
    return jax.shard_map(
        functools.partial(local, mesh.shape["text"], mesh.shape["video"]),
        mesh=mesh,
        in_specs=placed,
        out_specs=(
            P("text", "video"),
            P("text", "video"),
            P(("video", "text"), None),
            P(("video", "text"), None),
        ),
        check_vma=False,
    )
```

```python
import functools
import math

import jax
import jax.numpy as jnp
from jax import lax
from jax.experimental import pallas as pl
from jax.experimental.pallas import tpu as pltpu
from jax.sharding import PartitionSpec as P

H = 32
G = 4
HD = 128
PER_GROUP = H // G
CORES = 2
DEPTH = 4
FLOOR = -1e30
MESH = pl.DeviceIdType.MESH
NT = (((1,), (1,)), ((), ()))


def remote(src, dst, send, recv, text, video):
    return pltpu.make_async_remote_copy(
        src_ref=src,
        dst_ref=dst,
        send_sem=send,
        recv_sem=recv,
        device_id=(text, video),
        device_id_type=MESH,
    )


def kernel(
    T, V, q_ref, go_ref, k_ref, v_ref, pos_ref, span_ref,
    att_ref, dq_ref, dk_ref, dv_ref,
    q_s, go_s, kv_s, kv_out, kv_in, kv_all, bias, s_all, dp_own, p_all, ds_all,
    part, r_core, s_y, r_y, s_z, r_z, att_s, dq_s,
    load_sem, out_sem, kv_send, kv_recv, fw_send, fw_recv,
    c_send, c_recv, y_send, y_recv, z_send, z_recv,
):
    Z = DEPTH
    Y = T // (CORES * Z)
    heads = H // V
    groups = max(1, heads // PER_GROUP)
    gheads = heads // groups
    own = kv_s.shape[1]
    half = own // CORES
    gw = groups * HD
    R = own // T
    scale = HD ** -0.5
    f32, bf16 = jnp.float32, jnp.bfloat16

    t = lax.axis_index("text")
    v = lax.axis_index("video")
    c = lax.rem(t, CORES)
    y = lax.rem(t // CORES, Y)
    z = t // (CORES * Y)
    sib = t + 1 - 2 * c

    def text_at(zz, yy):
        return (zz * Y + yy) * CORES + c

    def key_column(rank):
        return pl.multiple_of(((rank * heads) // PER_GROUP) * HD, HD)

    def source(k):
        return lax.rem(v - k + V, V)

    loads = [
        pltpu.make_async_copy(k_ref, kv_s.at[0], load_sem.at[0]),
        pltpu.make_async_copy(v_ref, kv_s.at[1], load_sem.at[1]),
    ]
    for gi in range(groups):
        cols = pl.ds(pl.multiple_of((v * heads + gi * gheads) * HD, HD), gheads * HD)
        loads.append(pltpu.make_async_copy(q_ref.at[:, cols], q_s.at[gi], load_sem.at[2 + 2 * gi]))
        loads.append(pltpu.make_async_copy(go_ref.at[:, cols], go_s.at[gi], load_sem.at[3 + 2 * gi]))
    for load in loads:
        load.start()

    barrier = pltpu.get_barrier_semaphore()
    partners = [(sib, v)]
    partners += [(text_at(z, lax.rem(y + k, Y)), v) for k in range(1, Y)]
    partners += [
        (text_at(lax.rem(z + k, Z), y), lax.rem(v + m, V)) for k in range(Z) for m in range(V) if k + m > 0
    ]
    for partner in partners:
        pl.semaphore_signal(barrier, inc=1, device_id=partner, device_id_type=MESH)

    loads[0].wait()
    loads[1].wait()
    rows = pl.ds(pl.multiple_of(c * half, half), half)
    rest = pl.ds(pl.multiple_of((1 - c) * half, half), half)
    for k in range(1, V):
        cols = pl.ds(key_column(lax.rem(v + k, V)), gw)
        for i in range(2):
            kv_out[i, k - 1] = kv_s[i, rows, cols].astype(f32)
    pl.semaphore_wait(barrier, len(partners))
    sends = [[], []]
    for i in range(2):
        for k in range(1, V):
            copy = remote(
                kv_out.at[i, k - 1], kv_in.at[i, k - 1, c], kv_send.at[i, k - 1], kv_recv.at[i, k - 1], t, lax.rem(v + k, V)
            )
            copy.start()
            sends[i].append(copy)
    forwards = [[], []]

    def forward(i):
        for k in range(1, V):
            sends[i][k - 1].wait_recv()
            copy = remote(
                kv_in.at[i, k - 1, c], kv_in.at[i, k - 1, c], fw_send.at[i, k - 1], fw_recv.at[i, k - 1], sib, v
            )
            copy.start()
            forwards[i].append(copy)
            kv_all[i, k, rows, :] = kv_in[i, k - 1, c]

    def collect(i):
        for k in range(1, V):
            forwards[i][k - 1].wait_recv()
            kv_all[i, k, rest, :] = kv_in[i, k - 1, 1 - c]

    pending = []
    flying = []

    def start_core(p):
        copy = remote(part.at[p, 1 - c], r_core.at[p], c_send.at[p], c_recv.at[p], sib, v)
        copy.start()
        return [copy]

    def start_y(p, before):
        before[0].wait_recv()
        s_y[p] = part[p, c] + r_core[p]
        copies = []
        for k in range(1, Y):
            yy = lax.rem(y + k, Y)
            copy = remote(s_y.at[p, yy], r_y.at[p, k - 1], y_send.at[p, k - 1], y_recv.at[p, k - 1], text_at(z, yy), v)
            copy.start()
            copies.append(copy)
        return copies

    def start_zx(p, before):
        total = s_y[p, y]
        for k in range(1, Y):
            before[k - 1].wait_recv()
            total += r_y[p, k - 1]
        s_z[p] = total
        copies = []
        for k in range(Z):
            for m in range(V):
                if k + m > 0:
                    zz, vv, at = lax.rem(z + k, Z), lax.rem(v + m, V), k * V + m - 1
                    copy = remote(
                        s_z.at[p, zz, vv], r_z.at[p, k, v], z_send.at[p, at], z_recv.at[p, at], text_at(zz, y), vv
                    )
                    copy.start()
                    copies.append(copy)
        r_z[p, 0, v] = s_z[p, z, v]
        return copies

    stages = (start_y, start_zx)

    def launch(p, grad):
        for j in range(V):
            for zz in range(Z):
                for yy in range(Y):
                    for cc in range(CORES):
                        at = j * own + ((zz * Y + yy) * CORES + cc) * R
                        part[p, cc, yy, zz, source(j)] = grad[at : at + R]
        flying.append([p, 0, start_core(p)])

    def tick():
        for piece in reversed(flying):
            p, stage, copies = piece
            if stage < len(stages):
                pending.extend(copies)
                piece[2] = stages[stage](p, copies)
                piece[1] = stage + 1

    pos = pos_ref[...]
    low = span_ref[0, 0]
    high = span_ref[0, 1]
    for j in range(V):
        token = source(j) * own + lax.broadcasted_iota(jnp.int32, (own, HD), 0)
        bias[j] = jnp.where((token >= low) & (token < high) & (token <= pos), 0.0, FLOOR)
    cols = pl.ds(key_column(v), gw)
    for i in range(2):
        kv_all[i, 0] = kv_s[i, :, cols].astype(f32)
    for load in loads[2:]:
        load.wait()

    unit = min(4, gheads)
    units = gheads // unit

    def unit_columns(n):
        return slice(n * unit * HD, (n + 1) * unit * HD)

    def head_rows(ref, gi, first, count):
        return jnp.concatenate([ref[gi, :, h * HD : (h + 1) * HD] for h in range(first, first + count)], axis=0)

    def key_rows(i, gi, j):
        return kv_all[i, j, :, gi * HD : (gi + 1) * HD].astype(bf16)

    def scores(keys, queries, j):
        raw = lax.dot_general(keys, queries, NT, preferred_element_type=f32)
        return raw * (scale * math.log2(math.e)) + jnp.concatenate([bias[j]] * unit, axis=1)

    for gi in range(groups):
        keys = key_rows(0, gi, 0)
        values = key_rows(1, gi, 0)
        for n in range(units):
            there = unit_columns(n)
            s_all[gi, 0, :, there] = scores(keys, head_rows(q_s, gi, n * unit, unit), 0)
            dp_own[gi, :, there] = lax.dot_general(
                values, head_rows(go_s, gi, n * unit, unit), NT, preferred_element_type=f32
            )

    forward(0)
    collect(0)
    for gi in range(groups):
        keys = [key_rows(0, gi, j) for j in range(V)]
        for n in range(units):
            there = unit_columns(n)
            queries = head_rows(q_s, gi, n * unit, unit)
            s = [s_all[gi, 0, :, there]] + [scores(keys[j], queries, j) for j in range(1, V)]
            peak = functools.reduce(jnp.maximum, [jnp.max(x, axis=0, keepdims=True) for x in s])
            e = [jnp.exp2(x - peak) for x in s]
            inverse = 1.0 / sum(jnp.sum(x, axis=0, keepdims=True) for x in e)
            for j in range(V):
                prob = e[j] * inverse
                s_all[gi, j, :, there] = prob
                p_all[gi, j * own : (j + 1) * own, there] = prob.astype(bf16)
            if n == 0:
                tick()
        grad = jnp.dot(p_all[gi], head_rows(go_s, gi, 0, gheads), preferred_element_type=f32)
        launch(gi, grad)
        if gi == 0:
            forward(1)

    collect(1)
    for gi in range(groups):
        values = [key_rows(1, gi, j) for j in range(V)]
        for n in range(units):
            there = unit_columns(n)
            gp = head_rows(go_s, gi, n * unit, unit)
            dprob = [dp_own[gi, :, there]] + [
                lax.dot_general(values[j], gp, NT, preferred_element_type=f32) for j in range(1, V)
            ]
            prob = [s_all[gi, j, :, there] for j in range(V)]
            delta = sum(jnp.sum(prob[j] * dprob[j], axis=0, keepdims=True) for j in range(V))
            for j in range(V):
                ds_all[gi, j * own : (j + 1) * own, there] = (prob[j] * (dprob[j] - delta)).astype(bf16)
            if n == 0:
                tick()
        grad = jnp.dot(ds_all[gi], head_rows(q_s, gi, 0, gheads), preferred_element_type=f32) * scale
        launch(groups + gi, grad)

    outs = []
    for gi in range(groups):
        kt = jnp.concatenate([kv_all[0, j, :, gi * HD : (gi + 1) * HD].T for j in range(V)], axis=1).astype(bf16)
        vt = jnp.concatenate([kv_all[1, j, :, gi * HD : (gi + 1) * HD].T for j in range(V)], axis=1).astype(bf16)
        for n in range(units):
            there = unit_columns(n)
            out = jnp.dot(vt, p_all[gi, :, there], preferred_element_type=f32)
            dq = jnp.dot(kt, ds_all[gi, :, there], preferred_element_type=f32) * scale
            for i in range(unit):
                here = slice(i * HD, (i + 1) * HD)
                h = n * unit + i
                att_s[gi, :, h * HD : (h + 1) * HD] = out[:, here].T.astype(bf16)
                dq_s[gi, :, h * HD : (h + 1) * HD] = dq[:, here].T.astype(bf16)
            if n == 0:
                tick()
        cols = slice(gi * gheads * HD, (gi + 1) * gheads * HD)
        for i, (src, dst) in enumerate(((att_s, att_ref), (dq_s, dq_ref))):
            copy = pltpu.make_async_copy(src.at[gi], dst.at[:, cols], out_sem.at[gi, i])
            copy.start()
            outs.append(copy)

    for _ in stages:
        tick()
    for _, _, copies in flying:
        for copy in copies:
            copy.wait_recv()
        pending.extend(copies)
    for g in range(G):
        if V <= G:
            found = [(g % groups, g // groups)]
        else:
            share = V // G
            found = [(0, g * share + i) for i in range(share)]
        there = slice(g * HD, (g + 1) * HD)
        dv_ref[:, there] = sum(r_z[gi, k, rank] for gi, rank in found for k in range(Z)).astype(bf16)
        dk_ref[:, there] = sum(r_z[groups + gi, k, rank] for gi, rank in found for k in range(Z)).astype(bf16)
    for copy in pending + sends[0] + sends[1] + forwards[0] + forwards[1]:
        copy.wait_send()
    for copy in outs:
        copy.wait()


def hand_on(*refs):
    sources, results, held, sems = refs[:4], refs[4:8], refs[8:12], refs[12]
    arrivals, departures = [], []
    for i in range(4):
        chunk = max(32, sources[i].shape[0] // 4) if i < 2 else sources[i].shape[0]
        for n in range(sources[i].shape[0] // chunk):
            rows = pl.ds(n * chunk, chunk)
            arrivals.append(pltpu.make_async_copy(sources[i].at[rows], held[i].at[rows], sems.at[0, i, n]))
            departures.append(pltpu.make_async_copy(held[i].at[rows], results[i].at[rows], sems.at[1, i, n]))
    for copy in arrivals:
        copy.start()
    for arrival, departure in zip(arrivals, departures):
        arrival.wait()
        departure.start()
    for copy in departures:
        copy.wait()


def local(T, V, queries, video_keys, video_values, grad_out, positions, span_bounds):
    Z = DEPTH
    Y = T // (CORES * Z)
    rows = queries.shape[0]
    own = video_keys.shape[0]
    tokens = own * V
    heads = H // V
    groups = max(1, heads // PER_GROUP)
    gheads = heads // groups
    gw = groups * HD
    R = own // T
    f32, bf16 = jnp.float32, jnp.bfloat16
    dma = pltpu.SemaphoreType.DMA
    hbm = pl.BlockSpec(memory_space=pl.ANY)
    vmem = pl.BlockSpec(memory_space=pltpu.VMEM)
    smem = pl.BlockSpec(memory_space=pltpu.SMEM)
    pieces = 2 * groups
    scratch = [
        pltpu.VMEM((groups, rows, gheads * HD), bf16),
        pltpu.VMEM((groups, rows, gheads * HD), bf16),
        pltpu.VMEM((2, own, G * HD), bf16),
        pltpu.VMEM((2, V - 1, own // CORES, gw), f32),
        pltpu.VMEM((2, V - 1, CORES, own // CORES, gw), f32),
        pltpu.VMEM((2, V, own, gw), f32),
        pltpu.VMEM((V, own, rows), f32),
        pltpu.VMEM((groups, V, own, gheads * rows), f32),
        pltpu.VMEM((groups, own, gheads * rows), f32),
        pltpu.VMEM((groups, tokens, gheads * rows), bf16),
        pltpu.VMEM((groups, tokens, gheads * rows), bf16),
        pltpu.VMEM((pieces, CORES, Y, Z, V, R, HD), f32),
        pltpu.VMEM((pieces, Y, Z, V, R, HD), f32),
        pltpu.VMEM((pieces, Y, Z, V, R, HD), f32),
        pltpu.VMEM((pieces, Y - 1, Z, V, R, HD), f32),
        pltpu.VMEM((pieces, Z, V, R, HD), f32),
        pltpu.VMEM((pieces, Z, V, R, HD), f32),
        pltpu.VMEM((groups, rows, gheads * HD), bf16),
        pltpu.VMEM((groups, rows, gheads * HD), bf16),
        dma((2 + 2 * groups,)),
        dma((groups, 2)),
        dma((2, V - 1)), dma((2, V - 1)), dma((2, V - 1)), dma((2, V - 1)),
        dma((pieces,)), dma((pieces,)),
        dma((pieces, Y - 1)), dma((pieces, Y - 1)),
        dma((pieces, Z * V - 1)), dma((pieces, Z * V - 1)),
    ]
    shapes = (
        jax.ShapeDtypeStruct((rows, heads * HD), bf16),
        jax.ShapeDtypeStruct((rows, heads * HD), bf16),
        jax.ShapeDtypeStruct((R, G * HD), bf16),
        jax.ShapeDtypeStruct((R, G * HD), bf16),
    )
    results = pl.pallas_call(
        functools.partial(kernel, T, V),
        out_shape=shapes,
        in_specs=[hbm, hbm, hbm, hbm, vmem, smem],
        out_specs=(hbm, hbm, vmem, vmem),
        scratch_shapes=scratch,
        compiler_params=pltpu.CompilerParams(
            collective_id=0, has_side_effects=True, vmem_limit_bytes=56 * 1024 * 1024
        ),
        cost_estimate=pl.CostEstimate(
            flops=12 * rows * heads * tokens * HD,
            bytes_accessed=8 * rows * heads * HD + 4 * own * G * HD,
            transcendentals=rows * heads * tokens,
        ),
        name="attention",
    )(queries, grad_out, video_keys, video_values, positions.reshape(1, rows), span_bounds)
    return pl.pallas_call(
        hand_on,
        out_shape=shapes,
        in_specs=[hbm] * 4,
        out_specs=(hbm,) * 4,
        scratch_shapes=[pltpu.VMEM(shape.shape, bf16) for shape in shapes] + [dma((2, 4, 4))],
        name="hand_on",
    )(*results)


def solution(mesh):
    placed = (
        P("text", None),
        P("video", None),
        P("video", None),
        P("text", None),
        P("text"),
        P("text", None),
    )
    return jax.shard_map(
        functools.partial(local, mesh.shape["text"], mesh.shape["video"]),
        mesh=mesh,
        in_specs=placed,
        out_specs=(
            P("text", "video"),
            P("text", "video"),
            P(("video", "text"), None),
            P(("video", "text"), None),
        ),
        check_vma=False,
    )
```

```python
import functools
import math

import jax
import jax.numpy as jnp
from jax import lax
from jax.experimental import pallas as pl
from jax.experimental.pallas import tpu as pltpu
from jax.sharding import PartitionSpec as P

H = 32
G = 4
HD = 128
PER_GROUP = H // G
CORES = 2
DEPTH = 4
FLOOR = -1e30
MESH = pl.DeviceIdType.MESH
NT = (((1,), (1,)), ((), ()))


def remote(src, dst, send, recv, text, video):
    return pltpu.make_async_remote_copy(
        src_ref=src,
        dst_ref=dst,
        send_sem=send,
        recv_sem=recv,
        device_id=(text, video),
        device_id_type=MESH,
    )


def kernel(
    T, V, q_ref, go_ref, k_ref, v_ref, pos_ref, span_ref,
    att_ref, dq_ref, dk_ref, dv_ref,
    q_s, go_s, kv_s, kv_out, kv_in, kv_all, bias, s_all, dp_own, own_peak, own_total, weights, p_all, ds_all,
    part, r_core, s_y, r_y, s_z, r_z, att_s, dq_s,
    load_sem, out_sem, kv_send, kv_recv, fw_send, fw_recv,
    c_send, c_recv, y_send, y_recv, z_send, z_recv,
):
    Z = DEPTH
    Y = T // (CORES * Z)
    heads = H // V
    groups = max(1, heads // PER_GROUP)
    gheads = heads // groups
    own = kv_s.shape[1]
    half = own // CORES
    gw = groups * HD
    R = own // T
    scale = HD ** -0.5
    f32, bf16 = jnp.float32, jnp.bfloat16

    t = lax.axis_index("text")
    v = lax.axis_index("video")
    c = lax.rem(t, CORES)
    y = lax.rem(t // CORES, Y)
    z = t // (CORES * Y)
    sib = t + 1 - 2 * c

    def text_at(zz, yy):
        return (zz * Y + yy) * CORES + c

    def key_column(rank):
        return pl.multiple_of(((rank * heads) // PER_GROUP) * HD, HD)

    def source(k):
        return lax.rem(v - k + V, V)

    loads = [
        pltpu.make_async_copy(k_ref, kv_s.at[0], load_sem.at[0]),
        pltpu.make_async_copy(v_ref, kv_s.at[1], load_sem.at[1]),
    ]
    for gi in range(groups):
        cols = pl.ds(pl.multiple_of((v * heads + gi * gheads) * HD, HD), gheads * HD)
        loads.append(pltpu.make_async_copy(q_ref.at[:, cols], q_s.at[gi], load_sem.at[2 + 2 * gi]))
        loads.append(pltpu.make_async_copy(go_ref.at[:, cols], go_s.at[gi], load_sem.at[3 + 2 * gi]))
    for load in loads:
        load.start()

    barrier = pltpu.get_barrier_semaphore()
    partners = [(sib, v)]
    partners += [(text_at(z, lax.rem(y + k, Y)), v) for k in range(1, Y)]
    partners += [
        (text_at(lax.rem(z + k, Z), y), lax.rem(v + m, V)) for k in range(Z) for m in range(V) if k + m > 0
    ]
    for partner in partners:
        pl.semaphore_signal(barrier, inc=1, device_id=partner, device_id_type=MESH)

    loads[0].wait()
    loads[1].wait()
    rows = pl.ds(pl.multiple_of(c * half, half), half)
    rest = pl.ds(pl.multiple_of((1 - c) * half, half), half)
    for k in range(1, V):
        cols = pl.ds(key_column(lax.rem(v + k, V)), gw)
        for i in range(2):
            kv_out[i, k - 1] = kv_s[i, rows, cols].astype(f32)
    pl.semaphore_wait(barrier, len(partners))
    sends = [[], []]
    for i in range(2):
        for k in range(1, V):
            copy = remote(
                kv_out.at[i, k - 1], kv_in.at[i, k - 1, c], kv_send.at[i, k - 1], kv_recv.at[i, k - 1], t, lax.rem(v + k, V)
            )
            copy.start()
            sends[i].append(copy)
    forwards = [[], []]

    def forward(i):
        for k in range(1, V):
            sends[i][k - 1].wait_recv()
            copy = remote(
                kv_in.at[i, k - 1, c], kv_in.at[i, k - 1, c], fw_send.at[i, k - 1], fw_recv.at[i, k - 1], sib, v
            )
            copy.start()
            forwards[i].append(copy)
            kv_all[i, k, rows, :] = kv_in[i, k - 1, c]

    def collect(i):
        for k in range(1, V):
            forwards[i][k - 1].wait_recv()
            kv_all[i, k, rest, :] = kv_in[i, k - 1, 1 - c]

    pending = []
    flying = []

    def start_core(p):
        copy = remote(part.at[p, 1 - c], r_core.at[p], c_send.at[p], c_recv.at[p], sib, v)
        copy.start()
        return [copy]

    def start_y(p, before):
        before[0].wait_recv()
        s_y[p] = part[p, c] + r_core[p]
        copies = []
        for k in range(1, Y):
            yy = lax.rem(y + k, Y)
            copy = remote(s_y.at[p, yy], r_y.at[p, k - 1], y_send.at[p, k - 1], y_recv.at[p, k - 1], text_at(z, yy), v)
            copy.start()
            copies.append(copy)
        return copies

    def start_zx(p, before):
        total = s_y[p, y]
        for k in range(1, Y):
            before[k - 1].wait_recv()
            total += r_y[p, k - 1]
        s_z[p] = total
        copies = []
        for k in range(Z):
            for m in range(V):
                if k + m > 0:
                    zz, vv, at = lax.rem(z + k, Z), lax.rem(v + m, V), k * V + m - 1
                    copy = remote(
                        s_z.at[p, zz, vv], r_z.at[p, k, v], z_send.at[p, at], z_recv.at[p, at], text_at(zz, y), vv
                    )
                    copy.start()
                    copies.append(copy)
        r_z[p, 0, v] = s_z[p, z, v]
        return copies

    stages = (start_y, start_zx)

    def launch(p, grad):
        for j in range(V):
            for zz in range(Z):
                for yy in range(Y):
                    for cc in range(CORES):
                        at = j * own + ((zz * Y + yy) * CORES + cc) * R
                        part[p, cc, yy, zz, source(j)] = grad[at : at + R]
        flying.append([p, 0, start_core(p)])

    def tick():
        for piece in reversed(flying):
            p, stage, copies = piece
            if stage < len(stages):
                pending.extend(copies)
                piece[2] = stages[stage](p, copies)
                piece[1] = stage + 1

    pos = pos_ref[...]
    low = span_ref[0, 0]
    high = span_ref[0, 1]
    for j in range(V):
        token = source(j) * own + lax.broadcasted_iota(jnp.int32, (own, HD), 0)
        bias[j] = jnp.where((token >= low) & (token < high) & (token <= pos), 0.0, FLOOR)
    cols = pl.ds(key_column(v), gw)
    for i in range(2):
        kv_all[i, 0] = kv_s[i, :, cols].astype(f32)
    for load in loads[2:]:
        load.wait()

    unit = min(4, gheads)
    units = gheads // unit

    def unit_columns(n):
        return slice(n * unit * HD, (n + 1) * unit * HD)

    def head_rows(ref, gi, first, count):
        return jnp.concatenate([ref[gi, :, h * HD : (h + 1) * HD] for h in range(first, first + count)], axis=0)

    def key_rows(i, gi, j):
        return kv_all[i, j, :, gi * HD : (gi + 1) * HD].astype(bf16)

    def scores(keys, queries, j):
        raw = lax.dot_general(keys, queries, NT, preferred_element_type=f32)
        return raw * (scale * math.log2(math.e)) + jnp.concatenate([bias[j]] * unit, axis=1)

    def exponentials(s):
        peak = jnp.max(s, axis=0, keepdims=True)
        e = jnp.exp2(s - peak)
        return e, peak, jnp.sum(e, axis=0, keepdims=True)

    for gi in range(groups):
        keys = key_rows(0, gi, 0)
        values = key_rows(1, gi, 0)
        for n in range(units):
            there = unit_columns(n)
            s_all[gi, 0, :, there], own_peak[gi, :, there], own_total[gi, :, there] = exponentials(
                scores(keys, head_rows(q_s, gi, n * unit, unit), 0)
            )
            dp_own[gi, :, there] = lax.dot_general(
                values, head_rows(go_s, gi, n * unit, unit), NT, preferred_element_type=f32
            )

    forward(0)
    collect(0)
    for gi in range(groups):
        keys = [key_rows(0, gi, j) for j in range(V)]
        for n in range(units):
            there = unit_columns(n)
            queries = head_rows(q_s, gi, n * unit, unit)
            e, peaks, totals = [None], [own_peak[gi, :, there]], [own_total[gi, :, there]]
            for j in range(1, V):
                block, peak, total = exponentials(scores(keys[j], queries, j))
                s_all[gi, j, :, there] = block
                e.append(block)
                peaks.append(peak)
                totals.append(total)
            e[0] = s_all[gi, 0, :, there]
            top = functools.reduce(jnp.maximum, peaks)
            shrink = [jnp.exp2(peak - top) for peak in peaks]
            inverse = 1.0 / sum(total * factor for total, factor in zip(totals, shrink))
            for j in range(V):
                weight = shrink[j] * inverse
                weights[gi, j, :, there] = weight
                p_all[gi, j * own : (j + 1) * own, there] = (e[j] * weight).astype(bf16)
            if n == 0:
                tick()
        grad = jnp.dot(p_all[gi], head_rows(go_s, gi, 0, gheads), preferred_element_type=f32)
        launch(gi, grad)
        if gi == 0:
            forward(1)

    collect(1)
    for gi in range(groups):
        values = [key_rows(1, gi, j) for j in range(V)]
        for n in range(units):
            there = unit_columns(n)
            gp = head_rows(go_s, gi, n * unit, unit)
            dprob = [dp_own[gi, :, there]] + [
                lax.dot_general(values[j], gp, NT, preferred_element_type=f32) for j in range(1, V)
            ]
            weight = [weights[gi, j, :, there] for j in range(V)]
            delta = sum(
                jnp.sum(s_all[gi, j, :, there] * dprob[j], axis=0, keepdims=True) * weight[j] for j in range(V)
            )
            for j in range(V):
                ds_all[gi, j * own : (j + 1) * own, there] = (
                    s_all[gi, j, :, there] * ((dprob[j] - delta) * weight[j])
                ).astype(bf16)
            if n == 0:
                tick()
        grad = jnp.dot(ds_all[gi], head_rows(q_s, gi, 0, gheads), preferred_element_type=f32) * scale
        launch(groups + gi, grad)

    outs = []
    for gi in range(groups):
        kt = jnp.concatenate([kv_all[0, j, :, gi * HD : (gi + 1) * HD].T for j in range(V)], axis=1).astype(bf16)
        vt = jnp.concatenate([kv_all[1, j, :, gi * HD : (gi + 1) * HD].T for j in range(V)], axis=1).astype(bf16)
        for n in range(units):
            there = unit_columns(n)
            out = jnp.dot(vt, p_all[gi, :, there], preferred_element_type=f32)
            dq = jnp.dot(kt, ds_all[gi, :, there], preferred_element_type=f32) * scale
            for i in range(unit):
                here = slice(i * HD, (i + 1) * HD)
                h = n * unit + i
                att_s[gi, :, h * HD : (h + 1) * HD] = out[:, here].T.astype(bf16)
                dq_s[gi, :, h * HD : (h + 1) * HD] = dq[:, here].T.astype(bf16)
            if n == 0:
                tick()
        cols = slice(gi * gheads * HD, (gi + 1) * gheads * HD)
        for i, (src, dst) in enumerate(((att_s, att_ref), (dq_s, dq_ref))):
            copy = pltpu.make_async_copy(src.at[gi], dst.at[:, cols], out_sem.at[gi, i])
            copy.start()
            outs.append(copy)

    for _ in stages:
        tick()
    for _, _, copies in flying:
        for copy in copies:
            copy.wait_recv()
        pending.extend(copies)
    for g in range(G):
        if V <= G:
            found = [(g % groups, g // groups)]
        else:
            share = V // G
            found = [(0, g * share + i) for i in range(share)]
        there = slice(g * HD, (g + 1) * HD)
        dv_ref[:, there] = sum(r_z[gi, k, rank] for gi, rank in found for k in range(Z)).astype(bf16)
        dk_ref[:, there] = sum(r_z[groups + gi, k, rank] for gi, rank in found for k in range(Z)).astype(bf16)
    for copy in pending + sends[0] + sends[1] + forwards[0] + forwards[1]:
        copy.wait_send()
    for copy in outs:
        copy.wait()


def hand_on(*refs):
    copies = [pltpu.make_async_copy(refs[i], refs[4 + i], refs[8].at[i]) for i in range(4)]
    for copy in copies:
        copy.start()
    for copy in copies:
        copy.wait()


def local(T, V, queries, video_keys, video_values, grad_out, positions, span_bounds):
    Z = DEPTH
    Y = T // (CORES * Z)
    rows = queries.shape[0]
    own = video_keys.shape[0]
    tokens = own * V
    heads = H // V
    groups = max(1, heads // PER_GROUP)
    gheads = heads // groups
    gw = groups * HD
    R = own // T
    f32, bf16 = jnp.float32, jnp.bfloat16
    dma = pltpu.SemaphoreType.DMA
    hbm = pl.BlockSpec(memory_space=pl.ANY)
    vmem = pl.BlockSpec(memory_space=pltpu.VMEM)
    smem = pl.BlockSpec(memory_space=pltpu.SMEM)
    pieces = 2 * groups
    scratch = [
        pltpu.VMEM((groups, rows, gheads * HD), bf16),
        pltpu.VMEM((groups, rows, gheads * HD), bf16),
        pltpu.VMEM((2, own, G * HD), bf16),
        pltpu.VMEM((2, V - 1, own // CORES, gw), f32),
        pltpu.VMEM((2, V - 1, CORES, own // CORES, gw), f32),
        pltpu.VMEM((2, V, own, gw), f32),
        pltpu.VMEM((V, own, rows), f32),
        pltpu.VMEM((groups, V, own, gheads * rows), f32),
        pltpu.VMEM((groups, own, gheads * rows), f32),
        pltpu.VMEM((groups, 1, gheads * rows), f32),
        pltpu.VMEM((groups, 1, gheads * rows), f32),
        pltpu.VMEM((groups, V, 1, gheads * rows), f32),
        pltpu.VMEM((groups, tokens, gheads * rows), bf16),
        pltpu.VMEM((groups, tokens, gheads * rows), bf16),
        pltpu.VMEM((pieces, CORES, Y, Z, V, R, HD), f32),
        pltpu.VMEM((pieces, Y, Z, V, R, HD), f32),
        pltpu.VMEM((pieces, Y, Z, V, R, HD), f32),
        pltpu.VMEM((pieces, Y - 1, Z, V, R, HD), f32),
        pltpu.VMEM((pieces, Z, V, R, HD), f32),
        pltpu.VMEM((pieces, Z, V, R, HD), f32),
        pltpu.VMEM((groups, rows, gheads * HD), bf16),
        pltpu.VMEM((groups, rows, gheads * HD), bf16),
        dma((2 + 2 * groups,)),
        dma((groups, 2)),
        dma((2, V - 1)), dma((2, V - 1)), dma((2, V - 1)), dma((2, V - 1)),
        dma((pieces,)), dma((pieces,)),
        dma((pieces, Y - 1)), dma((pieces, Y - 1)),
        dma((pieces, Z * V - 1)), dma((pieces, Z * V - 1)),
    ]
    shapes = (
        jax.ShapeDtypeStruct((rows, heads * HD), bf16),
        jax.ShapeDtypeStruct((rows, heads * HD), bf16),
        jax.ShapeDtypeStruct((R, G * HD), bf16),
        jax.ShapeDtypeStruct((R, G * HD), bf16),
    )
    results = pl.pallas_call(
        functools.partial(kernel, T, V),
        out_shape=tuple(pltpu.VMEM(shape.shape, bf16) for shape in shapes),
        in_specs=[hbm, hbm, hbm, hbm, vmem, smem],
        out_specs=(hbm, hbm, vmem, vmem),
        scratch_shapes=scratch,
        compiler_params=pltpu.CompilerParams(
            collective_id=0, has_side_effects=True, vmem_limit_bytes=56 * 1024 * 1024
        ),
        cost_estimate=pl.CostEstimate(
            flops=12 * rows * heads * tokens * HD,
            bytes_accessed=8 * rows * heads * HD + 4 * own * G * HD,
            transcendentals=rows * heads * tokens,
        ),
        name="attention",
    )(queries, grad_out, video_keys, video_values, positions.reshape(1, rows), span_bounds)
    return pl.pallas_call(
        hand_on,
        out_shape=shapes,
        in_specs=[hbm] * 4,
        out_specs=(hbm,) * 4,
        scratch_shapes=[dma((4,))],
        name="hand_on",
    )(*results)


def solution(mesh):
    placed = (
        P("text", None),
        P("video", None),
        P("video", None),
        P("text", None),
        P("text"),
        P("text", None),
    )
    return jax.shard_map(
        functools.partial(local, mesh.shape["text"], mesh.shape["video"]),
        mesh=mesh,
        in_specs=placed,
        out_specs=(
            P("text", "video"),
            P("text", "video"),
            P(("video", "text"), None),
            P(("video", "text"), None),
        ),
        check_vma=False,
    )
```

```python
import functools
import math

import jax
import jax.numpy as jnp
from jax import lax
from jax.experimental import pallas as pl
from jax.experimental.pallas import tpu as pltpu
from jax.sharding import PartitionSpec as P

H = 32
G = 4
HD = 128
PER_GROUP = H // G
CORES = 2
DEPTH = 4
FLOOR = -1e30
MESH = pl.DeviceIdType.MESH
NT = (((1,), (1,)), ((), ()))


def remote(src, dst, send, recv, text, video):
    return pltpu.make_async_remote_copy(
        src_ref=src,
        dst_ref=dst,
        send_sem=send,
        recv_sem=recv,
        device_id=(text, video),
        device_id_type=MESH,
    )


def kernel(
    T, V, q_ref, go_ref, k_ref, v_ref, pos_ref, span_ref,
    att_ref, dq_ref, dk_ref, dv_ref,
    q_s, go_s, kv_s, kv_out, kv_in, kv_all, bias, s_all, dp_own, own_peak, own_total, weights, p_all, ds_all,
    part, r_core, s_y, r_y, s_z, r_z, att_s, dq_s,
    load_sem, out_sem, kv_send, kv_recv, fw_send, fw_recv,
    c_send, c_recv, y_send, y_recv, z_send, z_recv,
):
    Z = DEPTH
    Y = T // (CORES * Z)
    heads = H // V
    groups = max(1, heads // PER_GROUP)
    gheads = heads // groups
    own = kv_s.shape[1]
    half = own // CORES
    R = own // T
    scale = HD ** -0.5
    f32, bf16 = jnp.float32, jnp.bfloat16

    t = lax.axis_index("text")
    v = lax.axis_index("video")
    c = lax.rem(t, CORES)
    y = lax.rem(t // CORES, Y)
    z = t // (CORES * Y)
    sib = t + 1 - 2 * c

    def text_at(zz, yy):
        return (zz * Y + yy) * CORES + c

    def key_column(rank, gi):
        return pl.multiple_of(((rank * heads) // PER_GROUP + gi) * HD, HD)

    def source(k):
        return lax.rem(v - k + V, V)

    loads = [
        pltpu.make_async_copy(k_ref, kv_s.at[0], load_sem.at[0]),
        pltpu.make_async_copy(v_ref, kv_s.at[1], load_sem.at[1]),
    ]
    for gi in range(groups):
        cols = pl.ds(pl.multiple_of((v * heads + gi * gheads) * HD, HD), gheads * HD)
        loads.append(pltpu.make_async_copy(q_ref.at[:, cols], q_s.at[gi], load_sem.at[2 + 2 * gi]))
        loads.append(pltpu.make_async_copy(go_ref.at[:, cols], go_s.at[gi], load_sem.at[3 + 2 * gi]))
    for load in loads:
        load.start()

    barrier = pltpu.get_barrier_semaphore()
    partners = [(sib, v)]
    partners += [(text_at(z, lax.rem(y + k, Y)), v) for k in range(1, Y)]
    partners += [
        (text_at(lax.rem(z + k, Z), y), lax.rem(v + m, V)) for k in range(Z) for m in range(V) if k + m > 0
    ]
    for partner in partners:
        pl.semaphore_signal(barrier, inc=1, device_id=partner, device_id_type=MESH)

    loads[0].wait()
    loads[1].wait()
    rows = pl.ds(pl.multiple_of(c * half, half), half)
    rest = pl.ds(pl.multiple_of((1 - c) * half, half), half)
    for i in range(2):
        for gi in range(groups):
            for k in range(1, V):
                kv_out[i, gi, k - 1] = kv_s[i, rows, pl.ds(key_column(lax.rem(v + k, V), gi), HD)].astype(f32)
    pl.semaphore_wait(barrier, len(partners))
    sends, forwards = {}, {}
    for i in range(2):
        for gi in range(groups):
            for k in range(1, V):
                at = (i, gi, k - 1)
                copy = remote(kv_out.at[at], kv_in.at[(*at, c)], kv_send.at[at], kv_recv.at[at], t, lax.rem(v + k, V))
                copy.start()
                sends[at] = copy

    def forward(i, gi):
        for k in range(1, V):
            at = (i, gi, k - 1)
            sends[at].wait_recv()
            copy = remote(kv_in.at[(*at, c)], kv_in.at[(*at, c)], fw_send.at[at], fw_recv.at[at], sib, v)
            copy.start()
            forwards[at] = copy
            kv_all[i, gi, k, rows, :] = kv_in[i, gi, k - 1, c]

    def collect(i, gi):
        for k in range(1, V):
            forwards[i, gi, k - 1].wait_recv()
            kv_all[i, gi, k, rest, :] = kv_in[i, gi, k - 1, 1 - c]

    pending = []
    flying = []

    def start_core(p):
        copy = remote(part.at[p, 1 - c], r_core.at[p], c_send.at[p], c_recv.at[p], sib, v)
        copy.start()
        return [copy]

    def start_y(p, before):
        before[0].wait_recv()
        s_y[p] = part[p, c] + r_core[p]
        copies = []
        for k in range(1, Y):
            yy = lax.rem(y + k, Y)
            copy = remote(s_y.at[p, yy], r_y.at[p, k - 1], y_send.at[p, k - 1], y_recv.at[p, k - 1], text_at(z, yy), v)
            copy.start()
            copies.append(copy)
        return copies

    def start_zx(p, before):
        total = s_y[p, y]
        for k in range(1, Y):
            before[k - 1].wait_recv()
            total += r_y[p, k - 1]
        s_z[p] = total
        copies = []
        for k in range(Z):
            for m in range(V):
                if k + m > 0:
                    zz, vv, at = lax.rem(z + k, Z), lax.rem(v + m, V), k * V + m - 1
                    copy = remote(
                        s_z.at[p, zz, vv], r_z.at[p, k, v], z_send.at[p, at], z_recv.at[p, at], text_at(zz, y), vv
                    )
                    copy.start()
                    copies.append(copy)
        r_z[p, 0, v] = s_z[p, z, v]
        return copies

    stages = (start_y, start_zx)

    def launch(p, grad):
        for j in range(V):
            for zz in range(Z):
                for yy in range(Y):
                    for cc in range(CORES):
                        at = j * own + ((zz * Y + yy) * CORES + cc) * R
                        part[p, cc, yy, zz, source(j)] = grad[at : at + R]
        flying.append([p, 0, start_core(p)])

    def tick():
        for piece in reversed(flying):
            p, stage, copies = piece
            if stage < len(stages):
                pending.extend(copies)
                piece[2] = stages[stage](p, copies)
                piece[1] = stage + 1

    pos = pos_ref[...]
    low = span_ref[0, 0]
    high = span_ref[0, 1]
    for j in range(V):
        token = source(j) * own + lax.broadcasted_iota(jnp.int32, (own, HD), 0)
        bias[j] = jnp.where((token >= low) & (token < high) & (token <= pos), 0.0, FLOOR)
    for i in range(2):
        for gi in range(groups):
            kv_all[i, gi, 0] = kv_s[i, :, pl.ds(key_column(v, gi), HD)].astype(f32)
    for load in loads[2:]:
        load.wait()

    unit = min(4, gheads)
    units = gheads // unit

    def unit_columns(n):
        return slice(n * unit * HD, (n + 1) * unit * HD)

    def head_rows(ref, gi, first, count):
        return jnp.concatenate([ref[gi, :, h * HD : (h + 1) * HD] for h in range(first, first + count)], axis=0)

    def key_rows(i, gi, j):
        return kv_all[i, gi, j].astype(bf16)

    def scores(keys, queries, j):
        raw = lax.dot_general(keys, queries, NT, preferred_element_type=f32)
        return raw * (scale * math.log2(math.e)) + jnp.concatenate([bias[j]] * unit, axis=1)

    def exponentials(s):
        peak = jnp.max(s, axis=0, keepdims=True)
        e = jnp.exp2(s - peak)
        return e, peak, jnp.sum(e, axis=0, keepdims=True)

    for gi in range(groups):
        keys = key_rows(0, gi, 0)
        values = key_rows(1, gi, 0)
        for n in range(units):
            there = unit_columns(n)
            s_all[gi, 0, :, there], own_peak[gi, :, there], own_total[gi, :, there] = exponentials(
                scores(keys, head_rows(q_s, gi, n * unit, unit), 0)
            )
            dp_own[gi, :, there] = lax.dot_general(
                values, head_rows(go_s, gi, n * unit, unit), NT, preferred_element_type=f32
            )

        forward(0, gi)

    for gi in range(groups):
        collect(0, gi)
        keys = [key_rows(0, gi, j) for j in range(V)]
        for n in range(units):
            there = unit_columns(n)
            queries = head_rows(q_s, gi, n * unit, unit)
            e, peaks, totals = [None], [own_peak[gi, :, there]], [own_total[gi, :, there]]
            for j in range(1, V):
                block, peak, total = exponentials(scores(keys[j], queries, j))
                s_all[gi, j, :, there] = block
                e.append(block)
                peaks.append(peak)
                totals.append(total)
            e[0] = s_all[gi, 0, :, there]
            top = functools.reduce(jnp.maximum, peaks)
            shrink = [jnp.exp2(peak - top) for peak in peaks]
            inverse = 1.0 / sum(total * factor for total, factor in zip(totals, shrink))
            for j in range(V):
                weight = shrink[j] * inverse
                weights[gi, j, :, there] = weight
                p_all[gi, j * own : (j + 1) * own, there] = (e[j] * weight).astype(bf16)
            if n == 0:
                tick()
        grad = jnp.dot(p_all[gi], head_rows(go_s, gi, 0, gheads), preferred_element_type=f32)
        launch(gi, grad)
        forward(1, gi)

    for gi in range(groups):
        collect(1, gi)
        values = [key_rows(1, gi, j) for j in range(V)]
        for n in range(units):
            there = unit_columns(n)
            gp = head_rows(go_s, gi, n * unit, unit)
            dprob = [dp_own[gi, :, there]] + [
                lax.dot_general(values[j], gp, NT, preferred_element_type=f32) for j in range(1, V)
            ]
            weight = [weights[gi, j, :, there] for j in range(V)]
            delta = sum(
                jnp.sum(s_all[gi, j, :, there] * dprob[j], axis=0, keepdims=True) * weight[j] for j in range(V)
            )
            for j in range(V):
                ds_all[gi, j * own : (j + 1) * own, there] = (
                    s_all[gi, j, :, there] * ((dprob[j] - delta) * weight[j])
                ).astype(bf16)
            if n == 0:
                tick()
        grad = jnp.dot(ds_all[gi], head_rows(q_s, gi, 0, gheads), preferred_element_type=f32) * scale
        launch(groups + gi, grad)

    outs = []
    for gi in range(groups):
        kt = jnp.concatenate([kv_all[0, gi, j].T for j in range(V)], axis=1).astype(bf16)
        vt = jnp.concatenate([kv_all[1, gi, j].T for j in range(V)], axis=1).astype(bf16)
        for n in range(units):
            there = unit_columns(n)
            out = jnp.dot(vt, p_all[gi, :, there], preferred_element_type=f32)
            dq = jnp.dot(kt, ds_all[gi, :, there], preferred_element_type=f32) * scale
            for i in range(unit):
                here = slice(i * HD, (i + 1) * HD)
                h = n * unit + i
                att_s[gi, :, h * HD : (h + 1) * HD] = out[:, here].T.astype(bf16)
                dq_s[gi, :, h * HD : (h + 1) * HD] = dq[:, here].T.astype(bf16)
            if n == 0:
                tick()
        cols = slice(gi * gheads * HD, (gi + 1) * gheads * HD)
        for i, (src, dst) in enumerate(((att_s, att_ref), (dq_s, dq_ref))):
            copy = pltpu.make_async_copy(src.at[gi], dst.at[:, cols], out_sem.at[gi, i])
            copy.start()
            outs.append(copy)

    for _ in stages:
        tick()
    for _, _, copies in flying:
        for copy in copies:
            copy.wait_recv()
        pending.extend(copies)
    for g in range(G):
        if V <= G:
            found = [(g % groups, g // groups)]
        else:
            share = V // G
            found = [(0, g * share + i) for i in range(share)]
        there = slice(g * HD, (g + 1) * HD)
        dv_ref[:, there] = sum(r_z[gi, k, rank] for gi, rank in found for k in range(Z)).astype(bf16)
        dk_ref[:, there] = sum(r_z[groups + gi, k, rank] for gi, rank in found for k in range(Z)).astype(bf16)
    for copy in pending + list(sends.values()) + list(forwards.values()):
        copy.wait_send()
    for copy in outs:
        copy.wait()


def hand_on(*refs):
    copies = [pltpu.make_async_copy(refs[i], refs[4 + i], refs[8].at[i]) for i in range(4)]
    for copy in copies:
        copy.start()
    for copy in copies:
        copy.wait()


def local(T, V, queries, video_keys, video_values, grad_out, positions, span_bounds):
    Z = DEPTH
    Y = T // (CORES * Z)
    rows = queries.shape[0]
    own = video_keys.shape[0]
    tokens = own * V
    heads = H // V
    groups = max(1, heads // PER_GROUP)
    gheads = heads // groups
    R = own // T
    f32, bf16 = jnp.float32, jnp.bfloat16
    dma = pltpu.SemaphoreType.DMA
    hbm = pl.BlockSpec(memory_space=pl.ANY)
    vmem = pl.BlockSpec(memory_space=pltpu.VMEM)
    smem = pl.BlockSpec(memory_space=pltpu.SMEM)
    pieces = 2 * groups
    scratch = [
        pltpu.VMEM((groups, rows, gheads * HD), bf16),
        pltpu.VMEM((groups, rows, gheads * HD), bf16),
        pltpu.VMEM((2, own, G * HD), bf16),
        pltpu.VMEM((2, groups, V - 1, own // CORES, HD), f32),
        pltpu.VMEM((2, groups, V - 1, CORES, own // CORES, HD), f32),
        pltpu.VMEM((2, groups, V, own, HD), f32),
        pltpu.VMEM((V, own, rows), f32),
        pltpu.VMEM((groups, V, own, gheads * rows), f32),
        pltpu.VMEM((groups, own, gheads * rows), f32),
        pltpu.VMEM((groups, 1, gheads * rows), f32),
        pltpu.VMEM((groups, 1, gheads * rows), f32),
        pltpu.VMEM((groups, V, 1, gheads * rows), f32),
        pltpu.VMEM((groups, tokens, gheads * rows), bf16),
        pltpu.VMEM((groups, tokens, gheads * rows), bf16),
        pltpu.VMEM((pieces, CORES, Y, Z, V, R, HD), f32),
        pltpu.VMEM((pieces, Y, Z, V, R, HD), f32),
        pltpu.VMEM((pieces, Y, Z, V, R, HD), f32),
        pltpu.VMEM((pieces, Y - 1, Z, V, R, HD), f32),
        pltpu.VMEM((pieces, Z, V, R, HD), f32),
        pltpu.VMEM((pieces, Z, V, R, HD), f32),
        pltpu.VMEM((groups, rows, gheads * HD), bf16),
        pltpu.VMEM((groups, rows, gheads * HD), bf16),
        dma((2 + 2 * groups,)),
        dma((groups, 2)),
        dma((2, groups, V - 1)), dma((2, groups, V - 1)), dma((2, groups, V - 1)), dma((2, groups, V - 1)),
        dma((pieces,)), dma((pieces,)),
        dma((pieces, Y - 1)), dma((pieces, Y - 1)),
        dma((pieces, Z * V - 1)), dma((pieces, Z * V - 1)),
    ]
    shapes = (
        jax.ShapeDtypeStruct((rows, heads * HD), bf16),
        jax.ShapeDtypeStruct((rows, heads * HD), bf16),
        jax.ShapeDtypeStruct((R, G * HD), bf16),
        jax.ShapeDtypeStruct((R, G * HD), bf16),
    )
    results = pl.pallas_call(
        functools.partial(kernel, T, V),
        out_shape=tuple(pltpu.VMEM(shape.shape, bf16) for shape in shapes),
        in_specs=[hbm, hbm, hbm, hbm, vmem, smem],
        out_specs=(hbm, hbm, vmem, vmem),
        scratch_shapes=scratch,
        compiler_params=pltpu.CompilerParams(
            collective_id=0, has_side_effects=True, vmem_limit_bytes=56 * 1024 * 1024
        ),
        cost_estimate=pl.CostEstimate(
            flops=12 * rows * heads * tokens * HD,
            bytes_accessed=8 * rows * heads * HD + 4 * own * G * HD,
            transcendentals=rows * heads * tokens,
        ),
        name="attention",
    )(queries, grad_out, video_keys, video_values, positions.reshape(1, rows), span_bounds)
    return pl.pallas_call(
        hand_on,
        out_shape=shapes,
        in_specs=[hbm] * 4,
        out_specs=(hbm,) * 4,
        scratch_shapes=[dma((4,))],
        compiler_params=pltpu.CompilerParams(vmem_limit_bytes=1024 * 1024),
        name="hand_on",
    )(*results)


def solution(mesh):
    placed = (
        P("text", None),
        P("video", None),
        P("video", None),
        P("text", None),
        P("text"),
        P("text", None),
    )
    return jax.shard_map(
        functools.partial(local, mesh.shape["text"], mesh.shape["video"]),
        mesh=mesh,
        in_specs=placed,
        out_specs=(
            P("text", "video"),
            P("text", "video"),
            P(("video", "text"), None),
            P(("video", "text"), None),
        ),
        check_vma=False,
    )
```

```python
import functools
import math

import jax
import jax.numpy as jnp
from jax import lax
from jax.experimental import pallas as pl
from jax.experimental.pallas import tpu as pltpu
from jax.sharding import PartitionSpec as P

H = 32
G = 4
HD = 128
PER_GROUP = H // G
CORES = 2
DEPTH = 4
FLOOR = -1e30
MESH = pl.DeviceIdType.MESH
NT = (((1,), (1,)), ((), ()))


def remote(src, dst, send, recv, text, video):
    return pltpu.make_async_remote_copy(
        src_ref=src,
        dst_ref=dst,
        send_sem=send,
        recv_sem=recv,
        device_id=(text, video),
        device_id_type=MESH,
    )


def kernel(
    T, V, q_ref, go_ref, k_ref, v_ref, pos_ref, span_ref,
    att_ref, dq_ref, dk_ref, dv_ref,
    q_s, go_s, kv_s, kv_out, kv_in, kv_all, bias, s_all, dp_own, own_peak, own_total, weights, p_all, ds_all,
    part, r_core, s_y, r_y, s_z, r_z, att_s, dq_s,
    load_sem, out_sem, kv_send, kv_recv, fw_send, fw_recv,
    c_send, c_recv, y_send, y_recv, z_send, z_recv,
):
    Z = DEPTH
    Y = T // (CORES * Z)
    heads = H // V
    groups = max(1, heads // PER_GROUP)
    gheads = heads // groups
    own = kv_s.shape[1]
    half = own // CORES
    R = own // T
    scale = HD ** -0.5
    f32, bf16 = jnp.float32, jnp.bfloat16

    t = lax.axis_index("text")
    v = lax.axis_index("video")
    c = lax.rem(t, CORES)
    y = lax.rem(t // CORES, Y)
    z = t // (CORES * Y)
    sib = t + 1 - 2 * c

    def text_at(zz, yy):
        return (zz * Y + yy) * CORES + c

    def key_column(rank, gi):
        return pl.multiple_of(((rank * heads) // PER_GROUP + gi) * HD, HD)

    def source(k):
        return lax.rem(v - k + V, V)

    loads = [
        pltpu.make_async_copy(k_ref, kv_s.at[0], load_sem.at[0]),
        pltpu.make_async_copy(v_ref, kv_s.at[1], load_sem.at[1]),
    ]
    for gi in range(groups):
        cols = pl.ds(pl.multiple_of((v * heads + gi * gheads) * HD, HD), gheads * HD)
        loads.append(pltpu.make_async_copy(q_ref.at[:, cols], q_s.at[gi], load_sem.at[2 + 2 * gi]))
        loads.append(pltpu.make_async_copy(go_ref.at[:, cols], go_s.at[gi], load_sem.at[3 + 2 * gi]))
    for load in loads:
        load.start()

    barrier = pltpu.get_barrier_semaphore()
    partners = [(sib, v)]
    partners += [(text_at(z, lax.rem(y + k, Y)), v) for k in range(1, Y)]
    partners += [
        (text_at(lax.rem(z + k, Z), y), lax.rem(v + m, V)) for k in range(Z) for m in range(V) if k + m > 0
    ]
    for partner in partners:
        pl.semaphore_signal(barrier, inc=1, device_id=partner, device_id_type=MESH)

    loads[0].wait()
    loads[1].wait()
    rows = pl.ds(pl.multiple_of(c * half, half), half)
    rest = pl.ds(pl.multiple_of((1 - c) * half, half), half)
    for i in range(2):
        for gi in range(groups):
            for k in range(1, V):
                kv_out[i, gi, k - 1] = kv_s[i, rows, pl.ds(key_column(lax.rem(v + k, V), gi), HD)].astype(f32)
    pl.semaphore_wait(barrier, len(partners))
    sends, forwards = {}, {}
    for i in range(2):
        for gi in range(groups):
            for k in range(1, V):
                at = (i, gi, k - 1)
                copy = remote(kv_out.at[at], kv_in.at[(*at, c)], kv_send.at[at], kv_recv.at[at], t, lax.rem(v + k, V))
                copy.start()
                sends[at] = copy

    def forward(i, gi):
        for k in range(1, V):
            at = (i, gi, k - 1)
            sends[at].wait_recv()
            copy = remote(kv_in.at[(*at, c)], kv_in.at[(*at, c)], fw_send.at[at], fw_recv.at[at], sib, v)
            copy.start()
            forwards[at] = copy
            kv_all[i, gi, k, rows, :] = kv_in[i, gi, k - 1, c]

    def collect(i, gi):
        for k in range(1, V):
            forwards[i, gi, k - 1].wait_recv()
            kv_all[i, gi, k, rest, :] = kv_in[i, gi, k - 1, 1 - c]

    pending = []
    flying = []

    def start_core(p):
        copy = remote(part.at[p, 1 - c], r_core.at[p], c_send.at[p], c_recv.at[p], sib, v)
        copy.start()
        return [copy]

    def start_y(p, before):
        before[0].wait_recv()
        s_y[p] = part[p, c] + r_core[p]
        copies = []
        for k in range(1, Y):
            yy = lax.rem(y + k, Y)
            copy = remote(s_y.at[p, yy], r_y.at[p, k - 1], y_send.at[p, k - 1], y_recv.at[p, k - 1], text_at(z, yy), v)
            copy.start()
            copies.append(copy)
        return copies

    def start_zx(p, before):
        total = s_y[p, y]
        for k in range(1, Y):
            before[k - 1].wait_recv()
            total += r_y[p, k - 1]
        s_z[p] = total
        copies = []
        for k in range(Z):
            for m in range(V):
                if k + m > 0:
                    zz, vv, at = lax.rem(z + k, Z), lax.rem(v + m, V), k * V + m - 1
                    copy = remote(
                        s_z.at[p, zz, vv], r_z.at[p, k, v], z_send.at[p, at], z_recv.at[p, at], text_at(zz, y), vv
                    )
                    copy.start()
                    copies.append(copy)
        r_z[p, 0, v] = s_z[p, z, v]
        return copies

    stages = (start_y, start_zx)

    def launch(p, grad):
        for j in range(V):
            for zz in range(Z):
                for yy in range(Y):
                    for cc in range(CORES):
                        at = j * own + ((zz * Y + yy) * CORES + cc) * R
                        part[p, cc, yy, zz, source(j)] = grad[at : at + R]
        flying.append([p, 0, start_core(p)])

    def tick():
        for piece in reversed(flying):
            p, stage, copies = piece
            if stage < len(stages):
                pending.extend(copies)
                piece[2] = stages[stage](p, copies)
                piece[1] = stage + 1

    pos = pos_ref[...]
    low = span_ref[0, 0]
    high = span_ref[0, 1]
    for j in range(V):
        token = source(j) * own + lax.broadcasted_iota(jnp.int32, (own, HD), 0)
        bias[j] = jnp.where((token >= low) & (token < high) & (token <= pos), 0.0, FLOOR)
    for i in range(2):
        for gi in range(groups):
            kv_all[i, gi, 0] = kv_s[i, :, pl.ds(key_column(v, gi), HD)].astype(f32)
    for load in loads[2:]:
        load.wait()

    unit = min(4, gheads)
    units = gheads // unit

    def unit_columns(n):
        return slice(n * unit * HD, (n + 1) * unit * HD)

    def head_rows(ref, gi, first, count):
        return jnp.concatenate([ref[gi, :, h * HD : (h + 1) * HD] for h in range(first, first + count)], axis=0)

    def key_rows(i, gi, j):
        return kv_all[i, gi, j].astype(bf16)

    def scores(keys, queries, j):
        raw = lax.dot_general(keys, queries, NT, preferred_element_type=f32)
        return raw * (scale * math.log2(math.e)) + jnp.concatenate([bias[j]] * unit, axis=1)

    def exponentials(s):
        peak = jnp.max(s, axis=0, keepdims=True)
        e = jnp.exp2(s - peak)
        return e, peak, jnp.sum(e, axis=0, keepdims=True)

    for gi in range(groups):
        keys = key_rows(0, gi, 0)
        values = key_rows(1, gi, 0)
        for n in range(units):
            there = unit_columns(n)
            s_all[gi, 0, :, there], own_peak[gi, :, there], own_total[gi, :, there] = exponentials(
                scores(keys, head_rows(q_s, gi, n * unit, unit), 0)
            )
            dp_own[gi, :, there] = lax.dot_general(
                values, head_rows(go_s, gi, n * unit, unit), NT, preferred_element_type=f32
            )

        forward(0, gi)

    for gi in range(groups):
        collect(0, gi)
        keys = [key_rows(0, gi, j) for j in range(V)]
        grad = jnp.zeros((V * own, HD), f32)
        for n in range(units):
            there = unit_columns(n)
            queries = head_rows(q_s, gi, n * unit, unit)
            e, peaks, totals = [None], [own_peak[gi, :, there]], [own_total[gi, :, there]]
            for j in range(1, V):
                block, peak, total = exponentials(scores(keys[j], queries, j))
                s_all[gi, j, :, there] = block
                e.append(block)
                peaks.append(peak)
                totals.append(total)
            e[0] = s_all[gi, 0, :, there]
            top = functools.reduce(jnp.maximum, peaks)
            shrink = [jnp.exp2(peak - top) for peak in peaks]
            inverse = 1.0 / sum(total * factor for total, factor in zip(totals, shrink))
            for j in range(V):
                weight = shrink[j] * inverse
                weights[gi, j, :, there] = weight
                p_all[gi, j * own : (j + 1) * own, there] = (e[j] * weight).astype(bf16)
            grad += jnp.dot(p_all[gi, :, there], head_rows(go_s, gi, n * unit, unit), preferred_element_type=f32)
        tick()
        launch(gi, grad)
        forward(1, gi)

    for gi in range(groups):
        collect(1, gi)
        values = [key_rows(1, gi, j) for j in range(V)]
        grad = jnp.zeros((V * own, HD), f32)
        for n in range(units):
            there = unit_columns(n)
            gp = head_rows(go_s, gi, n * unit, unit)
            dprob = [dp_own[gi, :, there]] + [
                lax.dot_general(values[j], gp, NT, preferred_element_type=f32) for j in range(1, V)
            ]
            weight = [weights[gi, j, :, there] for j in range(V)]
            delta = sum(
                jnp.sum(s_all[gi, j, :, there] * dprob[j], axis=0, keepdims=True) * weight[j] for j in range(V)
            )
            for j in range(V):
                ds_all[gi, j * own : (j + 1) * own, there] = (
                    s_all[gi, j, :, there] * ((dprob[j] - delta) * weight[j])
                ).astype(bf16)
            grad += jnp.dot(ds_all[gi, :, there], head_rows(q_s, gi, n * unit, unit), preferred_element_type=f32)
        tick()
        launch(groups + gi, grad * scale)

    outs = []
    for gi in range(groups):
        kt = jnp.concatenate([kv_all[0, gi, j].T for j in range(V)], axis=1).astype(bf16)
        vt = jnp.concatenate([kv_all[1, gi, j].T for j in range(V)], axis=1).astype(bf16)
        for n in range(units):
            there = unit_columns(n)
            out = jnp.dot(vt, p_all[gi, :, there], preferred_element_type=f32)
            dq = jnp.dot(kt, ds_all[gi, :, there], preferred_element_type=f32) * scale
            for i in range(unit):
                here = slice(i * HD, (i + 1) * HD)
                h = n * unit + i
                att_s[gi, :, h * HD : (h + 1) * HD] = out[:, here].T.astype(bf16)
                dq_s[gi, :, h * HD : (h + 1) * HD] = dq[:, here].T.astype(bf16)
            if n == 0:
                tick()
        cols = slice(gi * gheads * HD, (gi + 1) * gheads * HD)
        for i, (src, dst) in enumerate(((att_s, att_ref), (dq_s, dq_ref))):
            copy = pltpu.make_async_copy(src.at[gi], dst.at[:, cols], out_sem.at[gi, i])
            copy.start()
            outs.append(copy)

    for _ in stages:
        tick()
    for _, _, copies in flying:
        for copy in copies:
            copy.wait_recv()
        pending.extend(copies)
    for g in range(G):
        if V <= G:
            found = [(g % groups, g // groups)]
        else:
            share = V // G
            found = [(0, g * share + i) for i in range(share)]
        there = slice(g * HD, (g + 1) * HD)
        dv_ref[:, there] = sum(r_z[gi, k, rank] for gi, rank in found for k in range(Z)).astype(bf16)
        dk_ref[:, there] = sum(r_z[groups + gi, k, rank] for gi, rank in found for k in range(Z)).astype(bf16)
    for copy in pending + list(sends.values()) + list(forwards.values()):
        copy.wait_send()
    for copy in outs:
        copy.wait()


def hand_on(*refs):
    copies = [pltpu.make_async_copy(refs[i], refs[4 + i], refs[8].at[i]) for i in range(4)]
    for copy in copies:
        copy.start()
    for copy in copies:
        copy.wait()


def local(T, V, queries, video_keys, video_values, grad_out, positions, span_bounds):
    Z = DEPTH
    Y = T // (CORES * Z)
    rows = queries.shape[0]
    own = video_keys.shape[0]
    tokens = own * V
    heads = H // V
    groups = max(1, heads // PER_GROUP)
    gheads = heads // groups
    R = own // T
    f32, bf16 = jnp.float32, jnp.bfloat16
    dma = pltpu.SemaphoreType.DMA
    hbm = pl.BlockSpec(memory_space=pl.ANY)
    vmem = pl.BlockSpec(memory_space=pltpu.VMEM)
    smem = pl.BlockSpec(memory_space=pltpu.SMEM)
    pieces = 2 * groups
    scratch = [
        pltpu.VMEM((groups, rows, gheads * HD), bf16),
        pltpu.VMEM((groups, rows, gheads * HD), bf16),
        pltpu.VMEM((2, own, G * HD), bf16),
        pltpu.VMEM((2, groups, V - 1, own // CORES, HD), f32),
        pltpu.VMEM((2, groups, V - 1, CORES, own // CORES, HD), f32),
        pltpu.VMEM((2, groups, V, own, HD), f32),
        pltpu.VMEM((V, own, rows), f32),
        pltpu.VMEM((groups, V, own, gheads * rows), f32),
        pltpu.VMEM((groups, own, gheads * rows), f32),
        pltpu.VMEM((groups, 1, gheads * rows), f32),
        pltpu.VMEM((groups, 1, gheads * rows), f32),
        pltpu.VMEM((groups, V, 1, gheads * rows), f32),
        pltpu.VMEM((groups, tokens, gheads * rows), bf16),
        pltpu.VMEM((groups, tokens, gheads * rows), bf16),
        pltpu.VMEM((pieces, CORES, Y, Z, V, R, HD), f32),
        pltpu.VMEM((pieces, Y, Z, V, R, HD), f32),
        pltpu.VMEM((pieces, Y, Z, V, R, HD), f32),
        pltpu.VMEM((pieces, Y - 1, Z, V, R, HD), f32),
        pltpu.VMEM((pieces, Z, V, R, HD), f32),
        pltpu.VMEM((pieces, Z, V, R, HD), f32),
        pltpu.VMEM((groups, rows, gheads * HD), bf16),
        pltpu.VMEM((groups, rows, gheads * HD), bf16),
        dma((2 + 2 * groups,)),
        dma((groups, 2)),
        dma((2, groups, V - 1)), dma((2, groups, V - 1)), dma((2, groups, V - 1)), dma((2, groups, V - 1)),
        dma((pieces,)), dma((pieces,)),
        dma((pieces, Y - 1)), dma((pieces, Y - 1)),
        dma((pieces, Z * V - 1)), dma((pieces, Z * V - 1)),
    ]
    shapes = (
        jax.ShapeDtypeStruct((rows, heads * HD), bf16),
        jax.ShapeDtypeStruct((rows, heads * HD), bf16),
        jax.ShapeDtypeStruct((R, G * HD), bf16),
        jax.ShapeDtypeStruct((R, G * HD), bf16),
    )
    results = pl.pallas_call(
        functools.partial(kernel, T, V),
        out_shape=tuple(pltpu.VMEM(shape.shape, bf16) for shape in shapes),
        in_specs=[hbm, hbm, hbm, hbm, vmem, smem],
        out_specs=(hbm, hbm, vmem, vmem),
        scratch_shapes=scratch,
        compiler_params=pltpu.CompilerParams(
            collective_id=0, has_side_effects=True, vmem_limit_bytes=56 * 1024 * 1024
        ),
        cost_estimate=pl.CostEstimate(
            flops=12 * rows * heads * tokens * HD,
            bytes_accessed=8 * rows * heads * HD + 4 * own * G * HD,
            transcendentals=rows * heads * tokens,
        ),
        name="attention",
    )(queries, grad_out, video_keys, video_values, positions.reshape(1, rows), span_bounds)
    return pl.pallas_call(
        hand_on,
        out_shape=shapes,
        in_specs=[hbm] * 4,
        out_specs=(hbm,) * 4,
        scratch_shapes=[dma((4,))],
        compiler_params=pltpu.CompilerParams(vmem_limit_bytes=1024 * 1024),
        name="hand_on",
    )(*results)


def solution(mesh):
    placed = (
        P("text", None),
        P("video", None),
        P("video", None),
        P("text", None),
        P("text"),
        P("text", None),
    )
    return jax.shard_map(
        functools.partial(local, mesh.shape["text"], mesh.shape["video"]),
        mesh=mesh,
        in_specs=placed,
        out_specs=(
            P("text", "video"),
            P("text", "video"),
            P(("video", "text"), None),
            P(("video", "text"), None),
        ),
        check_vma=False,
    )
```

```python
import functools
import math

import jax
import jax.numpy as jnp
from jax import lax
from jax.experimental import pallas as pl
from jax.experimental.pallas import tpu as pltpu
from jax.sharding import PartitionSpec as P

H = 32
G = 4
HD = 128
PER_GROUP = H // G
CORES = 2
DEPTH = 4
FLOOR = -1e30
MESH = pl.DeviceIdType.MESH
NT = (((1,), (1,)), ((), ()))


def remote(src, dst, send, recv, text, video):
    return pltpu.make_async_remote_copy(
        src_ref=src,
        dst_ref=dst,
        send_sem=send,
        recv_sem=recv,
        device_id=(text, video),
        device_id_type=MESH,
    )


def kernel(
    T, V, q_ref, go_ref, k_ref, v_ref, pos_ref, span_ref,
    att_ref, dq_ref, dk_ref, dv_ref,
    q_s, go_s, kv_s, kv_out, kv_in, kv_all, bias, s_all, dp_own, own_peak, own_total, weights, p_all, ds_all,
    part, r_core, s_y, r_y, s_z, r_z, att_s, dq_s,
    load_sem, out_sem, kv_send, kv_recv, fw_send, fw_recv,
    c_send, c_recv, y_send, y_recv, z_send, z_recv,
):
    Z = DEPTH
    Y = T // (CORES * Z)
    heads = H // V
    groups = max(1, heads // PER_GROUP)
    gheads = heads // groups
    own = kv_s.shape[1]
    half = own // CORES
    R = own // T
    scale = HD ** -0.5
    f32, bf16 = jnp.float32, jnp.bfloat16

    t = lax.axis_index("text")
    v = lax.axis_index("video")
    c = lax.rem(t, CORES)
    y = lax.rem(t // CORES, Y)
    z = t // (CORES * Y)
    sib = t + 1 - 2 * c

    def text_at(zz, yy):
        return (zz * Y + yy) * CORES + c

    def key_column(rank, gi):
        return pl.multiple_of(((rank * heads) // PER_GROUP + gi) * HD, HD)

    def source(k):
        return lax.rem(v - k + V, V)

    loads = [
        pltpu.make_async_copy(k_ref, kv_s.at[0], load_sem.at[0]),
        pltpu.make_async_copy(v_ref, kv_s.at[1], load_sem.at[1]),
    ]
    for gi in range(groups):
        cols = pl.ds(pl.multiple_of((v * heads + gi * gheads) * HD, HD), gheads * HD)
        loads.append(pltpu.make_async_copy(q_ref.at[:, cols], q_s.at[gi], load_sem.at[2 + 2 * gi]))
        loads.append(pltpu.make_async_copy(go_ref.at[:, cols], go_s.at[gi], load_sem.at[3 + 2 * gi]))
    for load in loads:
        load.start()

    barrier = pltpu.get_barrier_semaphore()
    partners = [(sib, v)]
    partners += [(text_at(z, lax.rem(y + k, Y)), v) for k in range(1, Y)]
    partners += [
        (text_at(lax.rem(z + k, Z), y), lax.rem(v + m, V)) for k in range(Z) for m in range(V) if k + m > 0
    ]
    for partner in partners:
        pl.semaphore_signal(barrier, inc=1, device_id=partner, device_id_type=MESH)

    loads[0].wait()
    loads[1].wait()
    rows = pl.ds(pl.multiple_of(c * half, half), half)
    rest = pl.ds(pl.multiple_of((1 - c) * half, half), half)
    for i in range(2):
        for gi in range(groups):
            for k in range(1, V):
                kv_out[i, gi, k - 1] = kv_s[i, rows, pl.ds(key_column(lax.rem(v + k, V), gi), HD)].astype(f32)
    pl.semaphore_wait(barrier, len(partners))
    sends, forwards = {}, {}
    for i in range(2):
        for gi in range(groups):
            for k in range(1, V):
                at = (i, gi, k - 1)
                copy = remote(kv_out.at[at], kv_in.at[(*at, c)], kv_send.at[at], kv_recv.at[at], t, lax.rem(v + k, V))
                copy.start()
                sends[at] = copy

    def forward(i, gi):
        for k in range(1, V):
            at = (i, gi, k - 1)
            sends[at].wait_recv()
            copy = remote(kv_in.at[(*at, c)], kv_in.at[(*at, c)], fw_send.at[at], fw_recv.at[at], sib, v)
            copy.start()
            forwards[at] = copy
            kv_all[i, gi, k, rows, :] = kv_in[i, gi, k - 1, c]

    def collect(i, gi):
        for k in range(1, V):
            forwards[i, gi, k - 1].wait_recv()
            kv_all[i, gi, k, rest, :] = kv_in[i, gi, k - 1, 1 - c]

    pending = []
    flying = []

    def start_core(p):
        copy = remote(part.at[p, 1 - c], r_core.at[p], c_send.at[p], c_recv.at[p], sib, v)
        copy.start()
        return [copy]

    def start_y(p, before):
        before[0].wait_recv()
        s_y[p] = part[p, c] + r_core[p]
        copies = []
        for k in range(1, Y):
            yy = lax.rem(y + k, Y)
            copy = remote(s_y.at[p, yy], r_y.at[p, k - 1], y_send.at[p, k - 1], y_recv.at[p, k - 1], text_at(z, yy), v)
            copy.start()
            copies.append(copy)
        return copies

    def start_zx(p, before):
        total = s_y[p, y]
        for k in range(1, Y):
            before[k - 1].wait_recv()
            total += r_y[p, k - 1]
        s_z[p] = total
        copies = []
        for k in range(Z):
            for m in range(V):
                if k + m > 0:
                    zz, vv, at = lax.rem(z + k, Z), lax.rem(v + m, V), k * V + m - 1
                    copy = remote(
                        s_z.at[p, zz, vv], r_z.at[p, k, v], z_send.at[p, at], z_recv.at[p, at], text_at(zz, y), vv
                    )
                    copy.start()
                    copies.append(copy)
        r_z[p, 0, v] = s_z[p, z, v]
        return copies

    stages = (start_y, start_zx)

    def launch(p, grad):
        for j in range(V):
            for zz in range(Z):
                for yy in range(Y):
                    for cc in range(CORES):
                        at = j * own + ((zz * Y + yy) * CORES + cc) * R
                        part[p, cc, yy, zz, source(j)] = grad[at : at + R]
        flying.append([p, 0, start_core(p)])

    def advance(piece):
        p, stage, copies = piece
        if stage < len(stages):
            pending.extend(copies)
            piece[2] = stages[stage](p, copies)
            piece[1] = stage + 1

    def tick():
        for piece in reversed(flying):
            advance(piece)

    def launch_between(p, grad):
        fresh = [piece for piece in flying if piece[1] == 0]
        older = [piece for piece in flying if piece[1] == 1]
        for piece in fresh:
            advance(piece)
        launch(p, grad)
        for piece in older:
            advance(piece)

    pos = pos_ref[...]
    low = span_ref[0, 0]
    high = span_ref[0, 1]
    for j in range(V):
        token = source(j) * own + lax.broadcasted_iota(jnp.int32, (own, HD), 0)
        bias[j] = jnp.where((token >= low) & (token < high) & (token <= pos), 0.0, FLOOR)
    for i in range(2):
        for gi in range(groups):
            kv_all[i, gi, 0] = kv_s[i, :, pl.ds(key_column(v, gi), HD)].astype(f32)
    for load in loads[2:]:
        load.wait()

    unit = min(4, gheads)
    units = gheads // unit

    def unit_columns(n):
        return slice(n * unit * HD, (n + 1) * unit * HD)

    def head_rows(ref, gi, first, count):
        return jnp.concatenate([ref[gi, :, h * HD : (h + 1) * HD] for h in range(first, first + count)], axis=0)

    def key_rows(i, gi, j):
        return kv_all[i, gi, j].astype(bf16)

    def scores(keys, queries, j):
        raw = lax.dot_general(keys, queries, NT, preferred_element_type=f32)
        return raw * (scale * math.log2(math.e)) + jnp.concatenate([bias[j]] * unit, axis=1)

    def exponentials(s):
        peak = jnp.max(s, axis=0, keepdims=True)
        e = jnp.exp2(s - peak)
        return e, peak, jnp.sum(e, axis=0, keepdims=True)

    for gi in range(groups):
        keys = key_rows(0, gi, 0)
        values = key_rows(1, gi, 0)
        for n in range(units):
            there = unit_columns(n)
            s_all[gi, 0, :, there], own_peak[gi, :, there], own_total[gi, :, there] = exponentials(
                scores(keys, head_rows(q_s, gi, n * unit, unit), 0)
            )
            dp_own[gi, :, there] = lax.dot_general(
                values, head_rows(go_s, gi, n * unit, unit), NT, preferred_element_type=f32
            )

        forward(0, gi)

    for gi in range(groups):
        collect(0, gi)
        keys = [key_rows(0, gi, j) for j in range(V)]
        grad = jnp.zeros((V * own, HD), f32)
        for n in range(units):
            there = unit_columns(n)
            queries = head_rows(q_s, gi, n * unit, unit)
            e, peaks, totals = [None], [own_peak[gi, :, there]], [own_total[gi, :, there]]
            for j in range(1, V):
                block, peak, total = exponentials(scores(keys[j], queries, j))
                s_all[gi, j, :, there] = block
                e.append(block)
                peaks.append(peak)
                totals.append(total)
            e[0] = s_all[gi, 0, :, there]
            top = functools.reduce(jnp.maximum, peaks)
            shrink = [jnp.exp2(peak - top) for peak in peaks]
            inverse = 1.0 / sum(total * factor for total, factor in zip(totals, shrink))
            for j in range(V):
                weight = shrink[j] * inverse
                weights[gi, j, :, there] = weight
                p_all[gi, j * own : (j + 1) * own, there] = (e[j] * weight).astype(bf16)
            grad += jnp.dot(p_all[gi, :, there], head_rows(go_s, gi, n * unit, unit), preferred_element_type=f32)
        launch_between(gi, grad)
        forward(1, gi)

    for gi in range(groups):
        collect(1, gi)
        values = [key_rows(1, gi, j) for j in range(V)]
        grad = jnp.zeros((V * own, HD), f32)
        for n in range(units):
            there = unit_columns(n)
            gp = head_rows(go_s, gi, n * unit, unit)
            dprob = [dp_own[gi, :, there]] + [
                lax.dot_general(values[j], gp, NT, preferred_element_type=f32) for j in range(1, V)
            ]
            weight = [weights[gi, j, :, there] for j in range(V)]
            delta = sum(
                jnp.sum(s_all[gi, j, :, there] * dprob[j], axis=0, keepdims=True) * weight[j] for j in range(V)
            )
            for j in range(V):
                ds_all[gi, j * own : (j + 1) * own, there] = (
                    s_all[gi, j, :, there] * ((dprob[j] - delta) * weight[j])
                ).astype(bf16)
            grad += jnp.dot(ds_all[gi, :, there], head_rows(q_s, gi, n * unit, unit), preferred_element_type=f32)
        launch_between(groups + gi, grad * scale)

    outs = []
    for gi in range(groups):
        kt = jnp.concatenate([kv_all[0, gi, j].T for j in range(V)], axis=1).astype(bf16)
        vt = jnp.concatenate([kv_all[1, gi, j].T for j in range(V)], axis=1).astype(bf16)
        for n in range(units):
            there = unit_columns(n)
            out = jnp.dot(vt, p_all[gi, :, there], preferred_element_type=f32)
            dq = jnp.dot(kt, ds_all[gi, :, there], preferred_element_type=f32) * scale
            for i in range(unit):
                here = slice(i * HD, (i + 1) * HD)
                h = n * unit + i
                att_s[gi, :, h * HD : (h + 1) * HD] = out[:, here].T.astype(bf16)
                dq_s[gi, :, h * HD : (h + 1) * HD] = dq[:, here].T.astype(bf16)
            if n == 0:
                tick()
        cols = slice(gi * gheads * HD, (gi + 1) * gheads * HD)
        for i, (src, dst) in enumerate(((att_s, att_ref), (dq_s, dq_ref))):
            copy = pltpu.make_async_copy(src.at[gi], dst.at[:, cols], out_sem.at[gi, i])
            copy.start()
            outs.append(copy)

    for _ in stages:
        tick()
    for _, _, copies in flying:
        for copy in copies:
            copy.wait_recv()
        pending.extend(copies)
    for g in range(G):
        if V <= G:
            found = [(g % groups, g // groups)]
        else:
            share = V // G
            found = [(0, g * share + i) for i in range(share)]
        there = slice(g * HD, (g + 1) * HD)
        dv_ref[:, there] = sum(r_z[gi, k, rank] for gi, rank in found for k in range(Z)).astype(bf16)
        dk_ref[:, there] = sum(r_z[groups + gi, k, rank] for gi, rank in found for k in range(Z)).astype(bf16)
    for copy in pending + list(sends.values()) + list(forwards.values()):
        copy.wait_send()
    for copy in outs:
        copy.wait()


def hand_on(*refs):
    copies = [pltpu.make_async_copy(refs[i], refs[4 + i], refs[8].at[i]) for i in range(4)]
    for copy in copies:
        copy.start()
    for copy in copies:
        copy.wait()


def local(T, V, queries, video_keys, video_values, grad_out, positions, span_bounds):
    Z = DEPTH
    Y = T // (CORES * Z)
    rows = queries.shape[0]
    own = video_keys.shape[0]
    tokens = own * V
    heads = H // V
    groups = max(1, heads // PER_GROUP)
    gheads = heads // groups
    R = own // T
    f32, bf16 = jnp.float32, jnp.bfloat16
    dma = pltpu.SemaphoreType.DMA
    hbm = pl.BlockSpec(memory_space=pl.ANY)
    vmem = pl.BlockSpec(memory_space=pltpu.VMEM)
    smem = pl.BlockSpec(memory_space=pltpu.SMEM)
    pieces = 2 * groups
    scratch = [
        pltpu.VMEM((groups, rows, gheads * HD), bf16),
        pltpu.VMEM((groups, rows, gheads * HD), bf16),
        pltpu.VMEM((2, own, G * HD), bf16),
        pltpu.VMEM((2, groups, V - 1, own // CORES, HD), f32),
        pltpu.VMEM((2, groups, V - 1, CORES, own // CORES, HD), f32),
        pltpu.VMEM((2, groups, V, own, HD), f32),
        pltpu.VMEM((V, own, rows), f32),
        pltpu.VMEM((groups, V, own, gheads * rows), f32),
        pltpu.VMEM((groups, own, gheads * rows), f32),
        pltpu.VMEM((groups, 1, gheads * rows), f32),
        pltpu.VMEM((groups, 1, gheads * rows), f32),
        pltpu.VMEM((groups, V, 1, gheads * rows), f32),
        pltpu.VMEM((groups, tokens, gheads * rows), bf16),
        pltpu.VMEM((groups, tokens, gheads * rows), bf16),
        pltpu.VMEM((pieces, CORES, Y, Z, V, R, HD), f32),
        pltpu.VMEM((pieces, Y, Z, V, R, HD), f32),
        pltpu.VMEM((pieces, Y, Z, V, R, HD), f32),
        pltpu.VMEM((pieces, Y - 1, Z, V, R, HD), f32),
        pltpu.VMEM((pieces, Z, V, R, HD), f32),
        pltpu.VMEM((pieces, Z, V, R, HD), f32),
        pltpu.VMEM((groups, rows, gheads * HD), bf16),
        pltpu.VMEM((groups, rows, gheads * HD), bf16),
        dma((2 + 2 * groups,)),
        dma((groups, 2)),
        dma((2, groups, V - 1)), dma((2, groups, V - 1)), dma((2, groups, V - 1)), dma((2, groups, V - 1)),
        dma((pieces,)), dma((pieces,)),
        dma((pieces, Y - 1)), dma((pieces, Y - 1)),
        dma((pieces, Z * V - 1)), dma((pieces, Z * V - 1)),
    ]
    shapes = (
        jax.ShapeDtypeStruct((rows, heads * HD), bf16),
        jax.ShapeDtypeStruct((rows, heads * HD), bf16),
        jax.ShapeDtypeStruct((R, G * HD), bf16),
        jax.ShapeDtypeStruct((R, G * HD), bf16),
    )
    results = pl.pallas_call(
        functools.partial(kernel, T, V),
        out_shape=tuple(pltpu.VMEM(shape.shape, bf16) for shape in shapes),
        in_specs=[hbm, hbm, hbm, hbm, vmem, smem],
        out_specs=(hbm, hbm, vmem, vmem),
        scratch_shapes=scratch,
        compiler_params=pltpu.CompilerParams(
            collective_id=0, has_side_effects=True, vmem_limit_bytes=56 * 1024 * 1024
        ),
        cost_estimate=pl.CostEstimate(
            flops=12 * rows * heads * tokens * HD,
            bytes_accessed=8 * rows * heads * HD + 4 * own * G * HD,
            transcendentals=rows * heads * tokens,
        ),
        name="attention",
    )(queries, grad_out, video_keys, video_values, positions.reshape(1, rows), span_bounds)
    return pl.pallas_call(
        hand_on,
        out_shape=shapes,
        in_specs=[hbm] * 4,
        out_specs=(hbm,) * 4,
        scratch_shapes=[dma((4,))],
        compiler_params=pltpu.CompilerParams(vmem_limit_bytes=1024 * 1024),
        name="hand_on",
    )(*results)


def solution(mesh):
    placed = (
        P("text", None),
        P("video", None),
        P("video", None),
        P("text", None),
        P("text"),
        P("text", None),
    )
    return jax.shard_map(
        functools.partial(local, mesh.shape["text"], mesh.shape["video"]),
        mesh=mesh,
        in_specs=placed,
        out_specs=(
            P("text", "video"),
            P("text", "video"),
            P(("video", "text"), None),
            P(("video", "text"), None),
        ),
        check_vma=False,
    )
```
